256 devices in a mesh: layer: 8 (over x, y_hi), group: 32 (over z, y_lo, core).
Axes of the slice: x: 4, y: 4 (y_hi: 2, y_lo: 2; y = y_hi * 2 + y_lo), z: 8, core: 2. Of those that a mesh axis runs over, the one named last changes fastest.
Arguments:
- activations: bfloat16 [16, 64, 64, 4096], P('layer', 'group'), may hold values from -6 to 6
- out_grads: bfloat16 [16, 64, 64, 4096], P('layer', 'group'), may hold values from -0.09375 to 0.09375
- in_factor: bfloat16 [16, 4096, 32], P('layer'), may hold values from -0.09375 to 0.09375
- out_factor: bfloat16 [16, 4096, 32], P('layer'), may hold values from -0.09375 to 0.09375
- stored_rows: bfloat16 [32768, 16, 1024], P('group', 'layer'), may hold values from -0.5390625 to 0.5390625
- example_class: int32 [64], P('group'), may hold values from 0 to 31
Outputs:
- self_gram: bfloat16 [32, 1024, 1024], P('group', 'layer')
- cross_gram: bfloat16 [32, 2, 1024, 1024], P('group', None, 'layer')
- class_scores: bfloat16 [32, 32768], P('layer', 'group')
The draws below stay inside these ranges and needn't reach their ends.
All inputs are finite; a program needn't handle non-finite values.
Results may differ from the reference program's by a relative error of at most 0.023.
Values may be sent and summed in bfloat16 or wider, within the bound.
A program may use at most 64 MiB of HBM per device.

```python
import jax
import jax.numpy as jnp
from jax import lax

D = 4096
RANK = 32
FEAT = 1024
LAYER_DEV = 2
LAYERS = 16
SEQ = 64
EXAMPLES = 64
CLASSES = 32
BLOCK = 1024
STORED = 32768
N_LAYER = 8
N_GROUP = 32


def plant(result, rng, least, top_value):
    longest = result.shape.index(max(result.shape))
    spots = []
    for shift in (0, 1):
        where = [jax.random.randint(jax.random.fold_in(rng, axis), (), 0, length) for axis, length in enumerate(result.shape)]
        where[longest] = (where[longest] + shift) % result.shape[longest]
        spots.append(tuple(where))
    return result.at[spots[0]].set(least).at[spots[1]].set(top_value)


def steps_of(stream_key, extent, cuts, low, largest):
    level = 1.0
    for axis_at, parts in cuts:
        steps = jax.random.uniform(jax.random.fold_in(jax.random.fold_in(stream_key, 6), axis_at), (parts,), jnp.float32, low / len(cuts), largest / len(cuts))
        level = level * jnp.repeat(jnp.exp(steps), extent[axis_at] // parts).reshape((-1,) + (1,) * (len(extent) - 1 - axis_at))
    return level


def scatter_about(stream_key, dims, spread, reach, cuts=(), held_as=jnp.bfloat16):
    level = steps_of(stream_key, dims, cuts, -0.22, 0.18) if cuts else 1.0
    drawn = jax.random.normal(stream_key, dims, jnp.float32) * spread * level
    return jnp.minimum(jnp.maximum(drawn, -reach), reach).astype(held_as)


def setup_inputs(seed: int = 0) -> dict:
    arg_keys = jax.random.split(jax.random.key(seed), 7)
    activations = scatter_about(arg_keys[0], (LAYERS, EXAMPLES, SEQ, D), 1.0, 6.0, ((0, 8), (1, 32)))
    out_grads = scatter_about(arg_keys[1], (LAYERS, EXAMPLES, SEQ, D), (SEQ * SEQ) ** -0.5, 0.09375, ((0, 8), (1, 32)))
    in_factor = scatter_about(arg_keys[2], (LAYERS, D, RANK), D ** -0.5, 0.09375, ((0, 8),))
    out_factor = scatter_about(arg_keys[3], (LAYERS, D, RANK), D ** -0.5, 0.09375, ((0, 8),))
    stored_rows = scatter_about(arg_keys[4], (STORED, LAYERS, FEAT), 0.09, 0.5390625, ((0, 32), (1, 8)))
    example_class = plant(jax.random.randint(arg_keys[5], (EXAMPLES,), 0, CLASSES), jax.random.fold_in(arg_keys[5], 1), 0, CLASSES - 1).astype(jnp.int32)
    return dict(activations=activations, out_grads=out_grads, in_factor=in_factor, out_factor=out_factor, stored_rows=stored_rows, example_class=example_class)


def slice_pair(left_rows, right_rows):
    total = jnp.zeros((left_rows.shape[0], right_rows.shape[0]), jnp.float32)
    for slice_index in range(N_LAYER):
        term = lax.dot_general(left_rows[:, slice_index], right_rows[:, slice_index], (((1,), (1,)), ((), ())), preferred_element_type=jnp.float32)
        rounded = lax.optimization_barrier(term.astype(jnp.bfloat16))
        total = total + rounded.astype(jnp.float32)
    return total


def reference(activations, out_grads, in_factor, out_factor, stored_rows, example_class):
    pieces = []
    for layer_index in range(LAYERS):
        left_side = jnp.dot(activations[layer_index].reshape(-1, D), in_factor[layer_index], preferred_element_type=jnp.float32).reshape(EXAMPLES, SEQ, RANK)
        right_side = jnp.dot(out_grads[layer_index].reshape(-1, D), out_factor[layer_index], preferred_element_type=jnp.float32).reshape(EXAMPLES, SEQ, RANK)
        outer = jnp.einsum('etp,etq->epq', left_side, right_side, precision=lax.Precision.HIGHEST)
        pieces.append(outer.reshape(EXAMPLES, RANK * RANK))
    fresh = jnp.concatenate(pieces, axis=1)
    one_hot = (example_class[:, None] == jnp.arange(CLASSES, dtype=jnp.int32)[None, :]).astype(jnp.float32)
    class_rows = jnp.dot(one_hot.T, fresh, precision=lax.Precision.HIGHEST, preferred_element_type=jnp.float32).astype(jnp.bfloat16)
    width = LAYER_DEV * RANK * RANK
    flat = stored_rows.reshape(STORED, N_LAYER, width)
    class_scores = slice_pair(class_rows.reshape(CLASSES, N_LAYER, width), flat).astype(jnp.bfloat16)
    blocks = flat.reshape(N_GROUP, BLOCK, N_LAYER, width)

    def one_block(block_index):
        own_block = blocks[block_index]
        near_block = blocks[(block_index + 1) % N_GROUP]
        far_block = blocks[(block_index + 2) % N_GROUP]
        tiles = jnp.stack([slice_pair(own_block, own_block), slice_pair(own_block, near_block), slice_pair(own_block, far_block)])
        return tiles.astype(jnp.bfloat16)

    all_tiles = lax.map(one_block, jnp.arange(N_GROUP, dtype=jnp.int32))
    return all_tiles[:, 0], all_tiles[:, 1:], class_scores
```

```python
import functools

import jax
import jax.numpy as jnp
from jax import lax
from jax.experimental import pallas as pl
from jax.experimental.pallas import tpu as pltpu
from jax.sharding import PartitionSpec as P

CLASSES = 32
MESH = pl.DeviceIdType.MESH
OWN, MATE, INNER, ALONG, CROSS = 0, 4, 8, 10, 12
PIECES = 9


def inner_block(left_rows, right_rows):
    return lax.dot_general(
        left_rows, right_rows, (((1,), (1,)), ((), ())), preferred_element_type=jnp.float32
    )


def tiles_kernel(
    own_hbm, self_ref, cross_ref,
    chunks, parts, hop, near_in, summed, home_self, home_near, home_far,
    own_sem, mate_s, mate_r, inner_s, inner_r, along_s, along_r, cross_s, cross_r,
    hop_s, hop_r, fold_s, fold_r, home_s, self_r, near_r, far_r,
):
    layer = lax.axis_index("layer")
    group = lax.axis_index("group")
    x, yh = layer // 2, layer % 2
    z, yl, core = group // 4, (group // 2) % 2, group % 2
    other = 1 - yh

    def at(xx, hh, gg):
        return (lax.rem(xx + 4, 4) * 2 + hh, lax.rem(gg + 32, 32))

    right, left = at(x + 1, yh, group), at(x - 1, yh, group)
    mirror = at(x, other, group)
    mate = at(x, yh, group + 1 - 2 * core)
    across = at(x, yh, group + 2 - 4 * yl)
    onward = at(x, yh, group + 4 - 8 * yl)
    greeted = [right, left, mirror]
    for step in (1, -1, 2, -2):
        greeted += [at(x, yh, group + step), at(x, other, group + step)]
    greeted += [at(x, yh, group + 4), at(x, yh, group - 4)]
    barrier = pltpu.get_barrier_semaphore()
    for who in greeted:
        pl.semaphore_signal(barrier, inc=1, device_id=who, device_id_type=MESH)
    own_copies = [
        pltpu.make_async_copy(own_hbm.at[k], chunks.at[pl.ds(OWN + 2 * k, 2)], own_sem.at[k])
        for k in range(2)
    ]
    for copy in own_copies:
        copy.start()
    pl.semaphore_wait(barrier, len(greeted))

    def remote(src, dst, send, recv, who):
        return pltpu.make_async_remote_copy(
            src_ref=src, dst_ref=dst, send_sem=send, recv_sem=recv, device_id=who, device_id_type=MESH
        )

    def rows_of(step):
        return step // 4, pl.ds((step % 4) * 128, 128)

    def inner_copy(step):
        k, rows = rows_of(step)
        return remote(own_hbm.at[k, yl, rows], chunks.at[INNER + k, rows], inner_s.at[step], inner_r.at[step], across)

    def along_copy(step):
        k, rows = rows_of(step)
        return remote(
            chunks.at[INNER + k, rows], chunks.at[ALONG + k, rows], along_s.at[step], along_r.at[step], onward
        )

    def mate_copy(k):
        return remote(own_hbm.at[k], chunks.at[pl.ds(MATE + 2 * k, 2)], mate_s.at[k], mate_r.at[k], mate)

    passes_inner = yl == core
    passed = jnp.where(passes_inner, INNER, ALONG)

    def cross_copy(k):
        return remote(chunks.at[passed + k], chunks.at[CROSS + k], cross_s.at[k], cross_r.at[k], mate)

    def hop_copy(p, side):
        return remote(
            parts.at[p, lax.rem(x + 2, 4), side], hop.at[p, side], hop_s.at[p, side], hop_r.at[p, side],
            right if side == 0 else left,
        )

    def fold_copy(p, side):
        to = lax.rem(x + 1, 4) if side == 0 else lax.rem(x + 3, 4)
        return remote(
            parts.at[p, to], near_in.at[p, side], fold_s.at[p, side], fold_r.at[p, side],
            right if side == 0 else left,
        )

    for step in range(8):
        inner_copy(step).start()
    mate_copy(0).start()

    @pl.when(core == 0)
    def _():
        mate_copy(1).start()

    def compute(p, left_slots, right_slots):
        for i in range(2):
            lefts, rights = left_slots(i), right_slots(i)

            def columns(n, carry):
                cols = pl.ds(pl.multiple_of(n * 256, 256), 256)
                total = None
                for a, b in zip(lefts, rights):
                    term = inner_block(chunks[a], chunks[b, cols, :])
                    total = term if total is None else total + term
                parts[p, :, i, :, cols] = total.astype(jnp.bfloat16).reshape(4, 128, 256)
                return carry

            lax.fori_loop(0, 2, columns, 0)
        for side in range(2):
            hop_copy(p, side).start()

    half = 1 - yl

    def half_piece(p, slot, is_row):
        def lefts(i):
            return [jnp.where(is_row, slot, OWN + 2 * i + half)]

        def rights(i):
            return [jnp.where(is_row, OWN + 2 * i + half, slot)]

        compute(p, lefts, rights)

    def fold(p):
        for side in range(2):
            to = lax.rem(x + 1, 4) if side == 0 else lax.rem(x + 3, 4)
            hop_copy(p, side).wait_recv()
            parts[p, to, side] = (
                parts[p, to, side].astype(jnp.float32) + hop[p, side].astype(jnp.float32)
            ).astype(jnp.bfloat16)
            fold_copy(p, side).start()

    def total_of(p):
        for side in range(2):
            fold_copy(p, side).wait_recv()
        summed[p] = (
            parts[p, x].astype(jnp.float32)
            + near_in[p, 0].astype(jnp.float32)
            + near_in[p, 1].astype(jnp.float32)
        ).astype(jnp.bfloat16)

    def self_home(k):
        return remote(summed.at[k, other], home_self.at[k], home_s.at[k, 0], self_r.at[k], mirror)

    def within_mirror():
        return remote(summed.at[2, other], home_near.at[0, 0], home_s.at[2, 0], near_r.at[0, 0], mirror)

    def within_mate():
        return remote(summed.at[2, yh], home_near.at[1, 1], home_s.at[2, 0], near_r.at[1, 1], mate)

    def within_mate_mirror():
        return remote(
            summed.at[2, other], home_near.at[2, 1], home_s.at[2, 1], near_r.at[2, 1],
            at(x, other, group + 1 - 2 * core),
        )

    def col_home(p, k, box, sems):
        return remote(summed.at[p, other], box.at[0, k], home_s.at[p, 0], sems.at[0, k], mirror)

    def row_home(p, k, box, sems, back):
        place = jnp.where(yh == k, 1, 2)
        return remote(summed.at[p], box.at[place], home_s.at[p, 0], sems.at[place, 0], at(x, k, group - back))

    def home_op(p, op):
        if p < 2:
            op(self_home(p))
        elif p == 2:

            @pl.when(core == 0)
            def _():
                op(within_mirror())

            @pl.when(core == 1)
            def _():
                op(within_mate())
                op(within_mate_mirror())
        else:
            k = (p - 3) % 2
            is_row = {0: yl == 1, 1: yl == 0, 2: core == 0}[(p - 3) // 2]
            box, sems, back = (home_far, far_r, 2) if p < 7 else (home_near, near_r, 1)

            @pl.when(is_row)
            def _():
                op(row_home(p, k, box, sems, back))

            @pl.when(jnp.logical_not(is_row))
            def _():
                op(col_home(p, k, box, sems))

    def finish(p):
        total_of(p)
        home_op(p, lambda copy: copy.start())

    def pass_on(step):
        inner_copy(step).wait_recv()
        along_copy(step).start()

    def take_along(k):
        for step in range(4 * k, 4 * k + 4):
            along_copy(step).wait_recv()

    def cross_inner(k):
        @pl.when(passes_inner)
        def _():
            cross_copy(k).start()

    def cross_along(k):
        @pl.when(jnp.logical_not(passes_inner))
        def _():
            cross_copy(k).start()

    def piece_inner(k):
        half_piece(3 + k, INNER + k, yl == 1)

    def piece_along(k):
        half_piece(5 + k, ALONG + k, yl == 0)

    def piece_cross(k):
        cross_copy(k).wait_recv()
        half_piece(7 + k, CROSS + k, core == 0)

    for copy in own_copies:
        copy.wait()
    for k in range(2):
        compute(k, lambda i: [OWN + 2 * i, OWN + 2 * i + 1], lambda i: [OWN + 2 * k, OWN + 2 * k + 1])
    pass_on(0)
    fold(0)
    mate_copy(0).wait_recv()

    @pl.when(core == 1)
    def _():
        mate_copy(1).wait_recv()

    theirs = jnp.where(core == 0, MATE, OWN + 2)
    compute(
        2,
        lambda i: [MATE * core + 2 * i, MATE * core + 2 * i + 1],
        lambda i: [theirs, theirs + 1],
    )
    fold(1)
    pass_on(1)
    finish(0)
    pass_on(2)
    fold(2)
    pass_on(3)
    cross_inner(0)
    piece_inner(0)
    finish(1)
    take_along(0)
    cross_along(0)
    piece_along(0)
    pass_on(4)
    fold(3)
    piece_cross(0)
    finish(2)
    pass_on(5)
    fold(5)
    fold(7)
    pass_on(6)
    finish(3)
    pass_on(7)
    cross_inner(1)
    piece_inner(1)
    finish(5)
    take_along(1)
    cross_along(1)
    piece_along(1)
    fold(4)
    piece_cross(1)
    finish(7)
    fold(6)
    fold(8)
    finish(4)
    finish(6)
    finish(8)

    def place(ref, k, value):
        for xv in range(4):
            ref[:, pl.ds(256 * xv + 128 * k, 128)] = value[:, 128 * xv : 128 * xv + 128].astype(jnp.bfloat16)

    def wide(value):
        return value.astype(jnp.float32)

    for k in range(2):
        self_home(k).wait_recv()
        place(self_ref.at[0], k, wide(summed[k, yh]) + wide(home_self[k]))

    @pl.when(core == 0)
    def _():
        within_mirror().wait_recv()
        place(cross_ref.at[0, 0], 0, wide(summed[2, yh]) + wide(home_near[0, 0]))
        remote(home_near.at[1, 1], home_near.at[1, 1], home_s.at[2, 0], near_r.at[1, 1], mate).wait_recv()
        remote(home_near.at[2, 1], home_near.at[2, 1], home_s.at[2, 0], near_r.at[2, 1], mate).wait_recv()
        place(cross_ref.at[0, 0], 1, wide(home_near[1, 1]) + wide(home_near[2, 1]))

    mine = jnp.where(yl == 0, 3, 5)

    def gather_home(box, sems, first, out):
        for k in range(2):
            remote(box.at[0, k], box.at[0, k], home_s.at[0, 0], sems.at[0, k], mirror).wait_recv()
        for source in (1, 2):
            remote(box.at[source], box.at[source], home_s.at[0, 0], sems.at[source, 0], mirror).wait_recv()
        for k in range(2):
            place(
                out, k,
                wide(summed[first + k, yh]) + wide(box[0, k]) + wide(box[1, k]) + wide(box[2, k]),
            )

    gather_home(home_far, far_r, mine, cross_ref.at[0, 1])

    @pl.when(core == 1)
    def _():
        gather_home(home_near, near_r, 7, cross_ref.at[0, 0])

    mate_copy(0).wait_send()

    @pl.when(core == 0)
    def _():
        mate_copy(1).wait_send()

    for step in range(8):
        inner_copy(step).wait_send()
        along_copy(step).wait_send()
    for k in range(2):
        cross_copy(k).wait_send()
    for p in range(PIECES):
        for side in range(2):
            hop_copy(p, side).wait_send()
            fold_copy(p, side).wait_send()
        home_op(p, lambda copy: copy.wait_send())


def gram_tiles(own):
    bf16 = jnp.bfloat16
    dma = pltpu.SemaphoreType.DMA
    return pl.pallas_call(
        tiles_kernel,
        out_shape=(
            jax.ShapeDtypeStruct((1, 128, 1024), bf16),
            jax.ShapeDtypeStruct((1, 2, 128, 1024), bf16),
        ),
        in_specs=[pl.BlockSpec(memory_space=pl.ANY)],
        out_specs=(pl.BlockSpec(memory_space=pltpu.VMEM), pl.BlockSpec(memory_space=pltpu.VMEM)),
        scratch_shapes=[
            pltpu.VMEM((14, 512, 1024), bf16),
            pltpu.VMEM((PIECES, 4, 2, 128, 512), bf16),
            pltpu.VMEM((PIECES, 2, 128, 512), bf16),
            pltpu.VMEM((PIECES, 2, 2, 128, 512), bf16),
            pltpu.VMEM((PIECES, 2, 128, 512), bf16),
            pltpu.VMEM((2, 128, 512), bf16),
            pltpu.VMEM((3, 2, 128, 512), bf16),
            pltpu.VMEM((3, 2, 128, 512), bf16),
            dma((2,)), dma((2,)), dma((2,)), dma((8,)), dma((8,)), dma((8,)), dma((8,)), dma((2,)), dma((2,)),
            dma((PIECES, 2)), dma((PIECES, 2)), dma((PIECES, 2)), dma((PIECES, 2)), dma((PIECES, 2)),
            dma((2,)), dma((3, 2)), dma((3, 2)),
        ],
        compiler_params=pltpu.CompilerParams(
            collective_id=0, has_side_effects=True, vmem_limit_bytes=56 * 2**20
        ),
        cost_estimate=pl.CostEstimate(flops=13 * 10**9, bytes_accessed=8 * 2**20, transcendentals=0),
        name="gram_tiles",
    )(own)


def per_device(activations, out_grads, in_factor, out_factor, stored_rows, example_class):
    layer_count = activations.shape[0]
    example_count = activations.shape[1]
    token_count = activations.shape[2]
    model_width = activations.shape[3]
    factor_rank = in_factor.shape[2]
    row_count = stored_rows.shape[0]
    chunked = stored_rows.reshape(4, 2, 128, 2, 1024).transpose(1, 3, 0, 2, 4).reshape(2, 2, 512, 1024)
    self_out, cross_out = gram_tiles(chunked)
    pieces = []
    for layer_index in range(layer_count):
        left_side = jnp.dot(
            activations[layer_index].reshape(-1, model_width),
            in_factor[layer_index],
            preferred_element_type=jnp.float32,
        ).reshape(example_count, token_count, factor_rank)
        right_side = jnp.dot(
            out_grads[layer_index].reshape(-1, model_width),
            out_factor[layer_index],
            preferred_element_type=jnp.float32,
        ).reshape(example_count, token_count, factor_rank)
        outer = jnp.einsum("etp,etq->epq", left_side, right_side, precision=lax.Precision.HIGHEST)
        pieces.append(outer.reshape(example_count, factor_rank * factor_rank))
    fresh = jnp.concatenate(pieces, axis=1)
    one_hot = (example_class[:, None] == jnp.arange(CLASSES, dtype=jnp.int32)[None, :]).astype(
        jnp.float32
    )
    local_sums = jnp.dot(
        one_hot.T, fresh, precision=lax.Precision.HIGHEST, preferred_element_type=jnp.float32
    )
    class_sums = lax.psum(local_sums.astype(jnp.bfloat16), "group")
    score_part = inner_block(class_sums, stored_rows.reshape(row_count, -1))
    score_sums = lax.psum_scatter(
        score_part.astype(jnp.bfloat16), "layer", scatter_dimension=0, tiled=True
    )
    return (self_out, cross_out, score_sums.astype(jnp.bfloat16))


def solution(mesh):
    placed = (
        P("layer", "group", None, None),
        P("layer", "group", None, None),
        P("layer", None, None),
        P("layer", None, None),
        P("group", "layer", None),
        P("group"),
    )
    return jax.shard_map(
        per_device,
        mesh=mesh,
        in_specs=placed,
        out_specs=(P("group", "layer", None), P("group", None, "layer", None), P("layer", "group")),
        check_vma=False,
    )
```

```python
import functools

import jax
import jax.numpy as jnp
from jax import lax
from jax.experimental import pallas as pl
from jax.experimental.pallas import tpu as pltpu
from jax.sharding import PartitionSpec as P

RANK = 32
MESH = pl.DeviceIdType.MESH
OWN, MATE, INNER, ALONG, CROSS = 0, 4, 8, 10, 12
PIECES = 9


def inner_block(left_rows, right_rows):
    return lax.dot_general(
        left_rows, right_rows, (((1,), (1,)), ((), ())), preferred_element_type=jnp.float32
    )


def tiles_kernel(
    own_hbm, acts_hbm, grads_hbm, in_hbm, out_hbm, class_ref, self_ref, cross_ref, score_ref,
    chunks, parts, hop, near_in, summed, home_self, home_near, home_far,
    acts, grads, in_rows, out_rows, note, notes, class_rows,
    score_parts, score_hop, score_near, score_sum, score_home,
    load_sem, ring_s, ring_r, share_s, share_r, sc_hop_s, sc_hop_r, sc_fold_s, sc_fold_r, sc_home_s, sc_home_r,
    own_sem, mate_s, mate_r, inner_s, inner_r, along_s, along_r, cross_s, cross_r,
    hop_s, hop_r, fold_s, fold_r, home_s, self_r, near_r, far_r,
):
    layer = lax.axis_index("layer")
    group = lax.axis_index("group")
    x, yh = layer // 2, layer % 2
    z, yl, core = group // 4, (group // 2) % 2, group % 2
    other = 1 - yh

    def at(xx, hh, gg):
        return (lax.rem(xx + 4, 4) * 2 + hh, lax.rem(gg + 32, 32))

    right, left = at(x + 1, yh, group), at(x - 1, yh, group)
    mirror = at(x, other, group)
    mate = at(x, yh, group + 1 - 2 * core)
    across = at(x, yh, group + 2 - 4 * yl)
    onward = at(x, yh, group + 4 - 8 * yl)
    greeted = [right, left, mirror]
    for step in (1, -1, 2, -2):
        greeted += [at(x, yh, group + step), at(x, other, group + step)]
    greeted += [at(x, yh, group + 4 * step) for step in range(1, 8)]
    barrier = pltpu.get_barrier_semaphore()
    for who in greeted:
        pl.semaphore_signal(barrier, inc=1, device_id=who, device_id_type=MESH)
    own_copies = [
        pltpu.make_async_copy(own_hbm.at[k], chunks.at[pl.ds(OWN + 2 * k, 2)], own_sem.at[k])
        for k in range(2)
    ]
    loads = [
        pltpu.make_async_copy(src, dst, load_sem.at[k])
        for k, (src, dst) in enumerate(
            [(acts_hbm, acts), (grads_hbm, grads), (in_hbm, in_rows), (out_hbm, out_rows)]
        )
    ]
    for copy in own_copies + loads:
        copy.start()
    pl.semaphore_wait(barrier, len(greeted))

    def remote(src, dst, send, recv, who):
        return pltpu.make_async_remote_copy(
            src_ref=src, dst_ref=dst, send_sem=send, recv_sem=recv, device_id=who, device_id_type=MESH
        )

    def rows_of(step):
        return step // 4, pl.ds((step % 4) * 128, 128)

    def inner_copy(step):
        k, rows = rows_of(step)
        return remote(own_hbm.at[k, yl, rows], chunks.at[INNER + k, rows], inner_s.at[step], inner_r.at[step], across)

    def along_copy(step):
        k, rows = rows_of(step)
        return remote(
            chunks.at[INNER + k, rows], chunks.at[ALONG + k, rows], along_s.at[step], along_r.at[step], onward
        )

    def mate_copy(k):
        return remote(own_hbm.at[k], chunks.at[pl.ds(MATE + 2 * k, 2)], mate_s.at[k], mate_r.at[k], mate)

    passes_inner = yl == core
    passed = jnp.where(passes_inner, INNER, ALONG)

    def cross_copy(k):
        return remote(chunks.at[passed + k], chunks.at[CROSS + k], cross_s.at[k], cross_r.at[k], mate)

    def hop_copy(p, side):
        return remote(
            parts.at[p, lax.rem(x + 2, 4), side], hop.at[p, side], hop_s.at[p, side], hop_r.at[p, side],
            right if side == 0 else left,
        )

    def fold_copy(p, side):
        to = lax.rem(x + 1, 4) if side == 0 else lax.rem(x + 3, 4)
        return remote(
            parts.at[p, to], near_in.at[p, side], fold_s.at[p, side], fold_r.at[p, side],
            right if side == 0 else left,
        )

    for step in range(8):
        inner_copy(step).start()
    mate_copy(0).start()

    @pl.when(core == 0)
    def _():
        mate_copy(1).start()

    def compute(p, left_slots, right_slots):
        for i in range(2):
            lefts, rights = left_slots(i), right_slots(i)

            def columns(n, carry):
                cols = pl.ds(pl.multiple_of(n * 256, 256), 256)
                total = None
                for a, b in zip(lefts, rights):
                    term = inner_block(chunks[a], chunks[b, cols, :])
                    total = term if total is None else total + term
                parts[p, :, i, :, cols] = total.astype(jnp.bfloat16).reshape(4, 128, 256)
                return carry

            lax.fori_loop(0, 2, columns, 0)
        for side in range(2):
            hop_copy(p, side).start()

    half = 1 - yl

    def half_piece(p, slot, is_row):
        def lefts(i):
            return [jnp.where(is_row, slot, OWN + 2 * i + half)]

        def rights(i):
            return [jnp.where(is_row, OWN + 2 * i + half, slot)]

        compute(p, lefts, rights)

    def fold(p):
        for side in range(2):
            to = lax.rem(x + 1, 4) if side == 0 else lax.rem(x + 3, 4)
            hop_copy(p, side).wait_recv()
            parts[p, to, side] = (
                parts[p, to, side].astype(jnp.float32) + hop[p, side].astype(jnp.float32)
            ).astype(jnp.bfloat16)
            fold_copy(p, side).start()

    def total_of(p):
        for side in range(2):
            fold_copy(p, side).wait_recv()
        summed[p] = (
            parts[p, x].astype(jnp.float32)
            + near_in[p, 0].astype(jnp.float32)
            + near_in[p, 1].astype(jnp.float32)
        ).astype(jnp.bfloat16)

    def self_home(k):
        return remote(summed.at[k, other], home_self.at[k], home_s.at[k, 0], self_r.at[k], mirror)

    def within_mirror():
        return remote(summed.at[2, other], home_near.at[0, 0], home_s.at[2, 0], near_r.at[0, 0], mirror)

    def within_mate():
        return remote(summed.at[2, yh], home_near.at[1, 1], home_s.at[2, 0], near_r.at[1, 1], mate)

    def within_mate_mirror():
        return remote(
            summed.at[2, other], home_near.at[2, 1], home_s.at[2, 1], near_r.at[2, 1],
            at(x, other, group + 1 - 2 * core),
        )

    def col_home(p, k, box, sems):
        return remote(summed.at[p, other], box.at[0, k], home_s.at[p, 0], sems.at[0, k], mirror)

    def row_home(p, k, box, sems, back):
        place = jnp.where(yh == k, 1, 2)
        return remote(summed.at[p], box.at[place], home_s.at[p, 0], sems.at[place, 0], at(x, k, group - back))

    def home_op(p, op):
        if p < 2:
            op(self_home(p))
        elif p == 2:

            @pl.when(core == 0)
            def _():
                op(within_mirror())

            @pl.when(core == 1)
            def _():
                op(within_mate())
                op(within_mate_mirror())
        else:
            k = (p - 3) % 2
            is_row = {0: yl == 1, 1: yl == 0, 2: core == 0}[(p - 3) // 2]
            box, sems, back = (home_far, far_r, 2) if p < 7 else (home_near, near_r, 1)

            @pl.when(is_row)
            def _():
                op(row_home(p, k, box, sems, back))

            @pl.when(jnp.logical_not(is_row))
            def _():
                op(col_home(p, k, box, sems))

    def finish(p):
        total_of(p)
        home_op(p, lambda copy: copy.start())

    def pass_on(step):
        inner_copy(step).wait_recv()
        along_copy(step).start()

    def take_along(k):
        for step in range(4 * k, 4 * k + 4):
            along_copy(step).wait_recv()

    def cross_inner(k):
        @pl.when(passes_inner)
        def _():
            cross_copy(k).start()

    def cross_along(k):
        @pl.when(jnp.logical_not(passes_inner))
        def _():
            cross_copy(k).start()

    def piece_inner(k):
        half_piece(3 + k, INNER + k, yl == 1)

    def piece_along(k):
        half_piece(5 + k, ALONG + k, yl == 0)

    def piece_cross(k):
        cross_copy(k).wait_recv()
        half_piece(7 + k, CROSS + k, core == 0)

    def ring_copy(step):
        return remote(
            notes.at[0, 0], notes.at[0, step], ring_s.at[step - 1], ring_r.at[step - 1],
            at(x, yh, group + 4 * step),
        )

    def share_copy(k):
        source, place, who = [(0, 2, across), (0, 1, mate), (2, 3, mate)][k]
        return remote(notes.at[source], notes.at[place], share_s.at[k], share_r.at[k], who)

    def exact_spread(value, spread):
        total = None
        for _ in range(3):
            part = value.astype(jnp.bfloat16)
            value = value - part.astype(jnp.float32)
            term = jnp.dot(part, spread, preferred_element_type=jnp.float32)
            total = term if total is None else total + term
        return total

    def project():
        for copy in loads:
            copy.wait()
        feature = lax.broadcasted_iota(jnp.int32, (RANK, RANK * RANK), 1)
        factor = lax.broadcasted_iota(jnp.int32, (RANK, RANK * RANK), 0)
        to_p = (feature // RANK == factor).astype(jnp.float32).astype(jnp.bfloat16)
        to_q = (feature % RANK == factor).astype(jnp.float32).astype(jnp.bfloat16)
        for k in range(2):
            left_side = exact_spread(inner_block(acts[k], in_rows[k]), to_p)
            right_side = exact_spread(inner_block(grads[k], out_rows[k]), to_q)
            outer = left_side * right_side
            for e in range(2):
                fresh = jnp.sum(outer[64 * e : 64 * e + 64], axis=0, keepdims=True)
                for c in range(4):
                    row = 8 * e + 4 * k + c
                    note[row : row + 1, 0:256] = fresh[:, 256 * c : 256 * c + 256]
        for e in range(2):
            note[8 * e : 8 * e + 8, 256:384] = jnp.full((8, 128), class_ref[e], jnp.int32).astype(jnp.float32)
        notes[0, 0] = note[...].astype(jnp.bfloat16)
        for step in range(1, 8):
            ring_copy(step).start()

    def share_first():
        for step in range(1, 8):
            ring_copy(step).wait_recv()
        share_copy(0).start()
        share_copy(1).start()

    def share_second():
        share_copy(0).wait_recv()
        share_copy(2).start()

    def score_hop_copy(side):
        return remote(
            score_parts.at[lax.rem(x + 2, 4), side], score_hop.at[side], sc_hop_s.at[side], sc_hop_r.at[side],
            right if side == 0 else left,
        )

    def score_fold_copy(side):
        to = lax.rem(x + 1, 4) if side == 0 else lax.rem(x + 3, 4)
        return remote(
            score_parts.at[to], score_near.at[side], sc_fold_s.at[side], sc_fold_r.at[side],
            right if side == 0 else left,
        )

    def score_home_copy():
        return remote(score_sum, score_home, sc_home_s, sc_home_r, mirror)

    def score_compute():
        share_copy(1).wait_recv()
        share_copy(2).wait_recv()
        rows = notes[...].reshape(512, 384)
        fresh = rows[:, 0:256]
        classes = rows[:, 256:384].astype(jnp.float32).T[0:64]
        spot = lax.broadcasted_iota(jnp.int32, (64, 512), 0)
        wanted = jnp.where(spot % 16 < 8, spot // 16 * 8 + spot % 16, -1).astype(jnp.float32)
        column = lax.broadcasted_iota(jnp.int32, (64, 512), 1) % 8
        for c in range(8):
            picked = jnp.where((classes == wanted) & (column == c), 1.0, 0.0).astype(jnp.bfloat16)
            class_rows[:, 256 * c : 256 * c + 256] = jnp.dot(
                picked, fresh, preferred_element_type=jnp.float32
            ).astype(jnp.bfloat16)
        for k in range(2):
            part = inner_block(class_rows[:, 0:1024], chunks[OWN + 2 * k]) + inner_block(
                class_rows[:, 1024:2048], chunks[OWN + 2 * k + 1]
            )
            score_parts[:, k] = part.astype(jnp.bfloat16).reshape(4, 16, 512)
        for side in range(2):
            score_hop_copy(side).start()

    def score_fold():
        for side in range(2):
            to = lax.rem(x + 1, 4) if side == 0 else lax.rem(x + 3, 4)
            score_hop_copy(side).wait_recv()
            score_parts[to, side] = (
                score_parts[to, side].astype(jnp.float32) + score_hop[side].astype(jnp.float32)
            ).astype(jnp.bfloat16)
            score_fold_copy(side).start()

    def score_finish():
        for side in range(2):
            score_fold_copy(side).wait_recv()
        score_sum[...] = (
            score_parts[x].astype(jnp.float32)
            + score_near[0].astype(jnp.float32)
            + score_near[1].astype(jnp.float32)
        ).astype(jnp.bfloat16)
        score_home_copy().start()

    for copy in own_copies:
        copy.wait()
    for k in range(2):
        compute(k, lambda i: [OWN + 2 * i, OWN + 2 * i + 1], lambda i: [OWN + 2 * k, OWN + 2 * k + 1])
    pass_on(0)
    fold(0)
    mate_copy(0).wait_recv()

    @pl.when(core == 1)
    def _():
        mate_copy(1).wait_recv()

    theirs = jnp.where(core == 0, MATE, OWN + 2)
    compute(
        2,
        lambda i: [MATE * core + 2 * i, MATE * core + 2 * i + 1],
        lambda i: [theirs, theirs + 1],
    )
    fold(1)
    pass_on(1)
    project()
    finish(0)
    pass_on(2)
    fold(2)
    share_first()
    pass_on(3)
    cross_inner(0)
    piece_inner(0)
    finish(1)
    take_along(0)
    cross_along(0)
    piece_along(0)
    share_second()
    pass_on(4)
    fold(3)
    piece_cross(0)
    score_compute()
    finish(2)
    pass_on(5)
    fold(5)
    fold(7)
    score_fold()
    pass_on(6)
    finish(3)
    pass_on(7)
    cross_inner(1)
    piece_inner(1)
    finish(5)
    score_finish()
    take_along(1)
    cross_along(1)
    piece_along(1)
    fold(4)
    piece_cross(1)
    finish(7)
    fold(6)
    fold(8)
    finish(4)
    finish(6)
    finish(8)

    def place(ref, k, value):
        for xv in range(4):
            ref[:, pl.ds(256 * xv + 128 * k, 128)] = value[:, 128 * xv : 128 * xv + 128].astype(jnp.bfloat16)

    def wide(value):
        return value.astype(jnp.float32)

    for k in range(2):
        self_home(k).wait_recv()
        place(self_ref.at[0], k, wide(summed[k, yh]) + wide(home_self[k]))

    @pl.when(core == 0)
    def _():
        within_mirror().wait_recv()
        place(cross_ref.at[0, 0], 0, wide(summed[2, yh]) + wide(home_near[0, 0]))
        remote(home_near.at[1, 1], home_near.at[1, 1], home_s.at[2, 0], near_r.at[1, 1], mate).wait_recv()
        remote(home_near.at[2, 1], home_near.at[2, 1], home_s.at[2, 0], near_r.at[2, 1], mate).wait_recv()
        place(cross_ref.at[0, 0], 1, wide(home_near[1, 1]) + wide(home_near[2, 1]))

    mine = jnp.where(yl == 0, 3, 5)

    def gather_home(box, sems, first, out):
        for k in range(2):
            remote(box.at[0, k], box.at[0, k], home_s.at[0, 0], sems.at[0, k], mirror).wait_recv()
        for source in (1, 2):
            remote(box.at[source], box.at[source], home_s.at[0, 0], sems.at[source, 0], mirror).wait_recv()
        for k in range(2):
            place(
                out, k,
                wide(summed[first + k, yh]) + wide(box[0, k]) + wide(box[1, k]) + wide(box[2, k]),
            )

    gather_home(home_far, far_r, mine, cross_ref.at[0, 1])

    @pl.when(core == 1)
    def _():
        gather_home(home_near, near_r, 7, cross_ref.at[0, 0])

    score_home_copy().wait_recv()
    for k in range(2):
        scores = wide(score_sum[k]) + wide(score_home[k])
        place(score_ref, k, jnp.where(yh == 0, scores[0:4], scores[4:8]))

    score_home_copy().wait_send()
    for side in range(2):
        score_hop_copy(side).wait_send()
        score_fold_copy(side).wait_send()
    for step in range(1, 8):
        ring_copy(step).wait_send()
    for k in range(3):
        share_copy(k).wait_send()
    mate_copy(0).wait_send()

    @pl.when(core == 0)
    def _():
        mate_copy(1).wait_send()

    for step in range(8):
        inner_copy(step).wait_send()
        along_copy(step).wait_send()
    for k in range(2):
        cross_copy(k).wait_send()
    for p in range(PIECES):
        for side in range(2):
            hop_copy(p, side).wait_send()
            fold_copy(p, side).wait_send()
        home_op(p, lambda copy: copy.wait_send())


def gram_tiles(own, acts, grads, in_rows, out_rows, classes):
    bf16 = jnp.bfloat16
    dma = pltpu.SemaphoreType.DMA
    return pl.pallas_call(
        tiles_kernel,
        out_shape=(
            jax.ShapeDtypeStruct((1, 128, 1024), bf16),
            jax.ShapeDtypeStruct((1, 2, 128, 1024), bf16),
            jax.ShapeDtypeStruct((4, 1024), bf16),
        ),
        in_specs=[pl.BlockSpec(memory_space=pl.ANY)] * 5 + [pl.BlockSpec(memory_space=pltpu.SMEM)],
        out_specs=(pl.BlockSpec(memory_space=pltpu.VMEM),) * 3,
        scratch_shapes=[
            pltpu.VMEM((14, 512, 1024), bf16),
            pltpu.VMEM((PIECES, 4, 2, 128, 512), bf16),
            pltpu.VMEM((PIECES, 2, 128, 512), bf16),
            pltpu.VMEM((PIECES, 2, 2, 128, 512), bf16),
            pltpu.VMEM((PIECES, 2, 128, 512), bf16),
            pltpu.VMEM((2, 128, 512), bf16),
            pltpu.VMEM((3, 2, 128, 512), bf16),
            pltpu.VMEM((3, 2, 128, 512), bf16),
            pltpu.VMEM((2, 128, 4096), bf16),
            pltpu.VMEM((2, 128, 4096), bf16),
            pltpu.VMEM((2, RANK, 4096), bf16),
            pltpu.VMEM((2, RANK, 4096), bf16),
            pltpu.VMEM((16, 384), jnp.float32),
            pltpu.VMEM((4, 8, 16, 384), bf16),
            pltpu.VMEM((64, 2048), bf16),
            pltpu.VMEM((4, 2, 16, 512), bf16),
            pltpu.VMEM((2, 16, 512), bf16),
            pltpu.VMEM((2, 2, 16, 512), bf16),
            pltpu.VMEM((2, 16, 512), bf16),
            pltpu.VMEM((2, 16, 512), bf16),
            dma((4,)), dma((7,)), dma((7,)), dma((3,)), dma((3,)),
            dma((2,)), dma((2,)), dma((2,)), dma((2,)), dma, dma,
            dma((2,)), dma((2,)), dma((2,)), dma((8,)), dma((8,)), dma((8,)), dma((8,)), dma((2,)), dma((2,)),
            dma((PIECES, 2)), dma((PIECES, 2)), dma((PIECES, 2)), dma((PIECES, 2)), dma((PIECES, 2)),
            dma((2,)), dma((3, 2)), dma((3, 2)),
        ],
        compiler_params=pltpu.CompilerParams(
            collective_id=0, has_side_effects=True, vmem_limit_bytes=56 * 2**20
        ),
        cost_estimate=pl.CostEstimate(flops=13 * 10**9, bytes_accessed=8 * 2**20, transcendentals=0),
        name="gram_tiles",
    )(own, acts, grads, in_rows, out_rows, classes)


def per_device(activations, out_grads, in_factor, out_factor, stored_rows, example_class):
    layer_count = activations.shape[0]
    model_width = activations.shape[3]
    chunked = stored_rows.reshape(4, 2, 128, 2, 1024).transpose(1, 3, 0, 2, 4).reshape(2, 2, 512, 1024)
    return gram_tiles(
        chunked,
        activations.reshape(layer_count, -1, model_width),
        out_grads.reshape(layer_count, -1, model_width),
        in_factor.transpose(0, 2, 1),
        out_factor.transpose(0, 2, 1),
        example_class,
    )


def solution(mesh):
    placed = (
        P("layer", "group", None, None),
        P("layer", "group", None, None),
        P("layer", None, None),
        P("layer", None, None),
        P("group", "layer", None),
        P("group"),
    )
    return jax.shard_map(
        per_device,
        mesh=mesh,
        in_specs=placed,
        out_specs=(P("group", "layer", None), P("group", None, "layer", None), P("layer", "group")),
        check_vma=False,
    )
```

```python
import functools

import jax
import jax.numpy as jnp
from jax import lax
from jax.experimental import pallas as pl
from jax.experimental.pallas import tpu as pltpu
from jax.sharding import PartitionSpec as P

RANK = 32
MESH = pl.DeviceIdType.MESH
OWN, MATE, INNER, ALONG, CROSS = 0, 4, 8, 10, 12
PIECES = 9


def inner_block(left_rows, right_rows):
    return lax.dot_general(
        left_rows, right_rows, (((1,), (1,)), ((), ())), preferred_element_type=jnp.float32
    )


def tiles_kernel(
    stored_hbm, acts_hbm, grads_hbm, in_hbm, out_hbm, class_ref, self_ref, cross_ref, score_ref,
    chunks, parts, hop, near_in, summed, home_self, home_near, home_far,
    acts, grads, in_rows, out_rows, note, notes, class_rows,
    score_parts, score_hop, score_near, score_sum, score_home,
    raw, turn_out, turn_in, turn_s, turn_r, load_sem, ring_s, ring_r, share_s, share_r, sc_hop_s, sc_hop_r, sc_fold_s, sc_fold_r, sc_home_s, sc_home_r,
    own_sem, mate_s, mate_r, inner_s, inner_r, along_s, along_r, cross_s, cross_r,
    hop_s, hop_r, fold_s, fold_r, home_s, self_r, near_r, far_r,
):
    layer = lax.axis_index("layer")
    group = lax.axis_index("group")
    x, yh = layer // 2, layer % 2
    z, yl, core = group // 4, (group // 2) % 2, group % 2
    other = 1 - yh

    def at(xx, hh, gg):
        return (lax.rem(xx + 4, 4) * 2 + hh, lax.rem(gg + 32, 32))

    right, left = at(x + 1, yh, group), at(x - 1, yh, group)
    mirror = at(x, other, group)
    mate = at(x, yh, group + 1 - 2 * core)
    across = at(x, yh, group + 2 - 4 * yl)
    onward = at(x, yh, group + 4 - 8 * yl)
    greeted = [right, left, mirror]
    for step in (1, -1, 2, -2):
        greeted += [at(x, yh, group + step), at(x, other, group + step)]
    greeted += [at(x, yh, group + 4 * step) for step in range(1, 8)]
    greeted += [at(x + step, other, group) for step in range(1, 4)]
    barrier = pltpu.get_barrier_semaphore()
    for who in greeted:
        pl.semaphore_signal(barrier, inc=1, device_id=who, device_id_type=MESH)
    own_copies = [
        pltpu.make_async_copy(stored_hbm.at[rows], raw.at[rows], own_sem.at[step])
        for step, rows in enumerate([pl.ds(256 * (step % 4) + 128 * (step // 4), 128) for step in range(8)])
    ]
    loads = [
        pltpu.make_async_copy(src, dst, load_sem.at[k])
        for k, (src, dst) in enumerate(
            [(acts_hbm, acts), (grads_hbm, grads), (in_hbm, in_rows), (out_hbm, out_rows)]
        )
    ]
    for copy in own_copies + loads:
        copy.start()
    pair = lax.broadcasted_iota(jnp.int32, (128, 256), 1)
    wanted_row = lax.broadcasted_iota(jnp.int32, (128, 256), 0) * 2
    pick = [(pair == wanted_row + f).astype(jnp.float32).astype(jnp.bfloat16) for f in range(2)]
    for copy in own_copies:
        copy.wait()

    def take_apart(step, carry):
        k, xv = step // 4, step % 4
        rows = raw[pl.ds(pl.multiple_of(256 * xv + 128 * k, 128), 128)].reshape(256, 1024)
        for f in range(2):
            chunks[OWN + 2 * k + f, pl.ds(pl.multiple_of(128 * xv, 128), 128), :] = jnp.dot(
                pick[f], rows, preferred_element_type=jnp.float32
            ).astype(jnp.bfloat16)
        return carry

    lax.fori_loop(0, 8, take_apart, 0)
    pl.semaphore_wait(barrier, len(greeted))

    def remote(src, dst, send, recv, who):
        return pltpu.make_async_remote_copy(
            src_ref=src, dst_ref=dst, send_sem=send, recv_sem=recv, device_id=who, device_id_type=MESH
        )

    def rows_of(step):
        return step // 4, pl.ds((step % 4) * 128, 128)

    def inner_copy(step):
        k, rows = rows_of(step)
        return remote(chunks.at[OWN + 2 * k + yl, rows], chunks.at[INNER + k, rows], inner_s.at[step], inner_r.at[step], across)

    def along_copy(step):
        k, rows = rows_of(step)
        return remote(
            chunks.at[INNER + k, rows], chunks.at[ALONG + k, rows], along_s.at[step], along_r.at[step], onward
        )

    def mate_copy(k):
        return remote(chunks.at[pl.ds(OWN + 2 * k, 2)], chunks.at[pl.ds(MATE + 2 * k, 2)], mate_s.at[k], mate_r.at[k], mate)

    passes_inner = yl == core
    passed = jnp.where(passes_inner, INNER, ALONG)

    def cross_copy(k):
        return remote(chunks.at[passed + k], chunks.at[CROSS + k], cross_s.at[k], cross_r.at[k], mate)

    def share(p, ref, h):
        if p == 0:
            return ref.at[h, :, pl.ds(0, 384)]
        if p == 1:
            return ref.at[0, :, pl.ds(256 * h, 256)]
        return ref.at[h]

    def hop_copy(p, side):
        return remote(
            share(p, parts.at[p, lax.rem(x + 2, 4)], side), share(p, hop.at[p], side),
            hop_s.at[p, side], hop_r.at[p, side], right if side == 0 else left,
        )

    def fold_copy(p, side, h):
        to = lax.rem(x + 1, 4) if side == 0 else lax.rem(x + 3, 4)
        return remote(
            share(p, parts.at[p, to], h), share(p, near_in.at[p, side], h),
            fold_s.at[p, side, h], fold_r.at[p, side, h], right if side == 0 else left,
        )

    for step in range(4):
        inner_copy(step).start()
    mate_copy(0).start()

    @pl.when(core == 0)
    def _():
        mate_copy(1).start()

    def send_shares(p):
        for side in range(2):
            hop_copy(p, side).start()
        for side in range(2):
            fold_copy(p, side, 1 - side).start()

    def product(lefts, rights, cols):
        total = None
        for a, b in zip(lefts, rights):
            term = inner_block(chunks[a], chunks[b, cols, :])
            total = term if total is None else total + term
        return total.astype(jnp.bfloat16).reshape(4, 128, 256)

    def diagonal():
        for i in range(2):
            slots = [OWN + 2 * i, OWN + 2 * i + 1]
            for n in range(2):
                total = product(slots, slots, pl.ds(256 * n, 256))
                for xu in range(4):
                    for xv in (2 * n, 2 * n + 1):
                        d = (xv - xu) % 4
                        if d < 3:
                            parts[0, xu, i, :, 128 * d : 128 * d + 128] = total[
                                xu, :, 128 * (xv - 2 * n) : 128 * (xv - 2 * n) + 128
                            ]
        send_shares(0)

    def compute(p, left_slots, right_slots):
        for i in range(1 if p == 1 else 2):
            lefts, rights = left_slots(i), right_slots(i)

            def columns(n, carry):
                cols = pl.ds(pl.multiple_of(n * 256, 256), 256)
                parts[p, :, i, :, cols] = product(lefts, rights, cols)
                return carry

            lax.fori_loop(0, 2, columns, 0)
        send_shares(p)

    half = 1 - yl

    def half_piece(p, slot, is_row):
        def lefts(i):
            return [jnp.where(is_row, slot, OWN + 2 * i + half)]

        def rights(i):
            return [jnp.where(is_row, OWN + 2 * i + half, slot)]

        compute(p, lefts, rights)

    def fold(p):
        for side in range(2):
            to = lax.rem(x + 1, 4) if side == 0 else lax.rem(x + 3, 4)
            hop_copy(p, side).wait_recv()
            mine, come = share(p, parts.at[p, to], side), share(p, hop.at[p], side)
            mine[...] = (mine[...].astype(jnp.float32) + come[...].astype(jnp.float32)).astype(jnp.bfloat16)
            fold_copy(p, side, side).start()

    def total_of(p, h):
        for side in range(2):
            fold_copy(p, side, h).wait_recv()
        share(p, summed.at[p], h)[...] = (
            share(p, parts.at[p, x], h)[...].astype(jnp.float32)
            + share(p, near_in.at[p, 0], h)[...].astype(jnp.float32)
            + share(p, near_in.at[p, 1], h)[...].astype(jnp.float32)
        ).astype(jnp.bfloat16)

    def diagonal_home(h):
        return remote(share(0, summed.at[0], h), home_self.at[0, :, pl.ds(0, 384)], home_s.at[0, h], self_r.at[0], mirror)

    def beside_home():
        return remote(summed.at[1, 0], home_self.at[1], home_s.at[1, 0], self_r.at[1], mirror)

    def turn_copy(xv):
        return remote(turn_out.at[xv], turn_in.at[x], turn_s.at[xv], turn_r.at[x], at(xv, 1, group))

    def next_copy():
        return remote(turn_out.at[4], turn_in.at[4], turn_s.at[4], turn_r.at[4], right)

    def within_mirror(h):
        return remote(summed.at[2, h], home_near.at[0, 0], home_s.at[2, h], near_r.at[0, 0], mirror)

    def within_mate(h):
        return remote(summed.at[2, h], home_near.at[1, 1], home_s.at[2, h], near_r.at[1, 1], mate)

    def within_mate_mirror(h):
        return remote(
            summed.at[2, h], home_near.at[2, 1], home_s.at[2, h], near_r.at[2, 1],
            at(x, other, group + 1 - 2 * core),
        )

    def col_home(p, k, h, box, sems):
        return remote(summed.at[p, h], box.at[0, k], home_s.at[p, h], sems.at[0, k], mirror)

    def row_home(p, k, h, box, sems, back):
        place = jnp.where(yh == k, 1, 2)
        return remote(
            summed.at[p, h], box.at[place, h], home_s.at[p, h], sems.at[place, h], at(x, k, group - back)
        )

    def home_op(p, h, op):
        if p == 0:

            @pl.when(other == h)
            def _():
                op(diagonal_home(h))
        elif p == 1:
            if h == 1:

                @pl.when(yh == 1)
                def _():
                    op(beside_home())
        elif p == 2:

            @pl.when((core == 0) & (other == h))
            def _():
                op(within_mirror(h))

            @pl.when((core == 1) & (yh == h))
            def _():
                op(within_mate(h))

            @pl.when((core == 1) & (other == h))
            def _():
                op(within_mate_mirror(h))
        else:
            k = (p - 3) % 2
            is_row = {0: yl == 1, 1: yl == 0, 2: core == 0}[(p - 3) // 2]
            box, sems, back = (home_far, far_r, 2) if p < 7 else (home_near, near_r, 1)

            @pl.when(is_row)
            def _():
                op(row_home(p, k, h, box, sems, back))

            @pl.when(jnp.logical_not(is_row) & (other == h))
            def _():
                op(col_home(p, k, h, box, sems))

    def finish(p):
        for h in range(2):
            total_of(p, h)
            home_op(p, h, lambda copy: copy.start())

    def pass_on(step):
        inner_copy(step).wait_recv()
        along_copy(step).start()
        if step < 4:
            inner_copy(step + 4).start()

    def take_along(k):
        for step in range(4 * k, 4 * k + 4):
            along_copy(step).wait_recv()

    def cross_inner(k):
        @pl.when(passes_inner)
        def _():
            cross_copy(k).start()

    def cross_along(k):
        @pl.when(jnp.logical_not(passes_inner))
        def _():
            cross_copy(k).start()

    def piece_inner(k):
        half_piece(3 + k, INNER + k, yl == 1)

    def piece_along(k):
        half_piece(5 + k, ALONG + k, yl == 0)

    def piece_cross(k):
        cross_copy(k).wait_recv()
        half_piece(7 + k, CROSS + k, core == 0)

    def over_copy():
        return remote(notes.at[0, 0, 0], notes.at[0, 0, 1], share_s.at[0], share_r.at[0], across)

    def ring_copy(step):
        return remote(
            notes.at[0, 0], notes.at[0, step], ring_s.at[step - 1], ring_r.at[step - 1],
            at(x, yh, group + 4 * step),
        )

    def note_mate_copy():
        return remote(notes.at[0], notes.at[1], share_s.at[1], share_r.at[1], mate)

    def exact_spread(value, spread):
        total = None
        for _ in range(3):
            part = value.astype(jnp.bfloat16)
            value = value - part.astype(jnp.float32)
            term = jnp.dot(part, spread, preferred_element_type=jnp.float32)
            total = term if total is None else total + term
        return total

    def project():
        for copy in loads:
            copy.wait()
        feature = lax.broadcasted_iota(jnp.int32, (RANK, RANK * RANK), 1)
        factor = lax.broadcasted_iota(jnp.int32, (RANK, RANK * RANK), 0)
        to_p = (feature // RANK == factor).astype(jnp.float32).astype(jnp.bfloat16)
        to_q = (feature % RANK == factor).astype(jnp.float32).astype(jnp.bfloat16)
        for k in range(2):
            left_side = exact_spread(inner_block(acts[k], in_rows[k]), to_p)
            right_side = exact_spread(inner_block(grads[k], out_rows[k]), to_q)
            outer = left_side * right_side
            for e in range(2):
                fresh = jnp.sum(outer[64 * e : 64 * e + 64], axis=0, keepdims=True)
                for c in range(4):
                    row = 8 * e + 4 * k + c
                    note[row : row + 1, 0:256] = fresh[:, 256 * c : 256 * c + 256]
        for e in range(2):
            note[8 * e : 8 * e + 8, 256:384] = jnp.full((8, 128), class_ref[e], jnp.int32).astype(jnp.float32)
        notes[0, 0, 0] = note[...].astype(jnp.bfloat16)
        over_copy().start()

    def share_first():
        over_copy().wait_recv()
        for step in range(1, 8):
            ring_copy(step).start()

    def share_second():
        for step in range(1, 8):
            ring_copy(step).wait_recv()
        note_mate_copy().start()

    def score_hop_copy(side):
        return remote(
            score_parts.at[lax.rem(x + 2, 4), side], score_hop.at[side], sc_hop_s.at[side], sc_hop_r.at[side],
            right if side == 0 else left,
        )

    def score_fold_copy(side):
        to = lax.rem(x + 1, 4) if side == 0 else lax.rem(x + 3, 4)
        return remote(
            score_parts.at[to], score_near.at[side], sc_fold_s.at[side], sc_fold_r.at[side],
            right if side == 0 else left,
        )

    def score_home_copy():
        return remote(score_sum, score_home, sc_home_s, sc_home_r, mirror)

    def score_compute():
        note_mate_copy().wait_recv()
        rows = notes[...].reshape(512, 384)
        fresh = rows[:, 0:256]
        classes = rows[:, 256:384].astype(jnp.float32).T[0:64]
        spot = lax.broadcasted_iota(jnp.int32, (64, 512), 0)
        wanted = jnp.where(spot % 16 < 8, spot // 16 * 8 + spot % 16, -1).astype(jnp.float32)
        column = lax.broadcasted_iota(jnp.int32, (64, 512), 1) % 8
        for c in range(8):
            picked = jnp.where((classes == wanted) & (column == c), 1.0, 0.0).astype(jnp.bfloat16)
            class_rows[:, 256 * c : 256 * c + 256] = jnp.dot(
                picked, fresh, preferred_element_type=jnp.float32
            ).astype(jnp.bfloat16)
        for k in range(2):
            part = inner_block(class_rows[:, 0:1024], chunks[OWN + 2 * k]) + inner_block(
                class_rows[:, 1024:2048], chunks[OWN + 2 * k + 1]
            )
            score_parts[:, k] = part.astype(jnp.bfloat16).reshape(4, 16, 512)
        for side in range(2):
            score_hop_copy(side).start()

    def score_fold():
        for side in range(2):
            to = lax.rem(x + 1, 4) if side == 0 else lax.rem(x + 3, 4)
            score_hop_copy(side).wait_recv()
            score_parts[to, side] = (
                score_parts[to, side].astype(jnp.float32) + score_hop[side].astype(jnp.float32)
            ).astype(jnp.bfloat16)
            score_fold_copy(side).start()

    def score_finish():
        for side in range(2):
            score_fold_copy(side).wait_recv()
        score_sum[...] = (
            score_parts[x].astype(jnp.float32)
            + score_near[0].astype(jnp.float32)
            + score_near[1].astype(jnp.float32)
        ).astype(jnp.bfloat16)
        score_home_copy().start()

    def place(ref, k, value):
        for xv in range(4):
            ref[:, pl.ds(256 * xv + 128 * k, 128)] = value[:, 128 * xv : 128 * xv + 128].astype(jnp.bfloat16)

    def wide(value):
        return value.astype(jnp.float32)

    def column(xv, k):
        return pl.ds(pl.multiple_of(256 * xv + 128 * k, 128), 128)

    def turn():
        remote(home_self.at[0, :, pl.ds(0, 384)], home_self.at[0, :, pl.ds(0, 384)], home_s.at[0, 0], self_r.at[0], mirror).wait_recv()
        diag = (wide(summed[0, yh, :, 0:384]) + wide(home_self[0, :, 0:384])).astype(jnp.bfloat16)
        for d in range(3):
            self_ref[0, :, column(lax.rem(x + d, 4), yh)] = diag[:, 128 * d : 128 * d + 128]
        turn_out[4] = diag[:, 128:256]
        next_copy().start()

        @pl.when(yh == 0)
        def _():
            beside_home().wait_recv()
            final = wide(summed[1, 0]) + wide(home_self[1])
            place(self_ref.at[0], 1, final)
            for xv in range(4):
                turn_out[xv] = final[:, 128 * xv : 128 * xv + 128].astype(jnp.bfloat16)
                turn_copy(xv).start()

    def turned():
        next_copy().wait_recv()
        self_ref[0, :, column(lax.rem(x + 3, 4), yh)] = wide(turn_in[4]).T.astype(jnp.bfloat16)

        @pl.when(yh == 1)
        def _():
            for xv in range(4):
                remote(turn_in.at[xv], turn_in.at[xv], turn_s.at[xv], turn_r.at[xv], mirror).wait_recv()
                self_ref[0, :, pl.ds(256 * xv, 128)] = wide(turn_in[xv]).T.astype(jnp.bfloat16)

    diagonal()
    compute(1, lambda i: [OWN, OWN + 1], lambda i: [OWN + 2, OWN + 3])
    project()
    pass_on(0)
    fold(0)
    mate_copy(0).wait_recv()

    @pl.when(core == 1)
    def _():
        mate_copy(1).wait_recv()

    theirs = jnp.where(core == 0, MATE, OWN + 2)
    compute(
        2,
        lambda i: [MATE * core + 2 * i, MATE * core + 2 * i + 1],
        lambda i: [theirs, theirs + 1],
    )
    fold(1)
    pass_on(1)
    fold(2)
    pass_on(2)
    pass_on(3)
    cross_inner(0)
    piece_inner(0)
    share_first()
    pass_on(4)
    take_along(0)
    cross_along(0)
    piece_along(0)
    fold(3)
    piece_cross(0)
    fold(5)
    pass_on(5)
    fold(7)
    pass_on(6)
    share_second()
    pass_on(7)
    cross_inner(1)
    piece_inner(1)
    score_compute()
    finish(0)
    finish(1)
    finish(2)
    finish(3)
    take_along(1)
    cross_along(1)
    piece_along(1)
    fold(4)
    score_fold()
    piece_cross(1)
    finish(5)
    fold(6)
    finish(7)
    fold(8)
    turn()
    score_finish()
    finish(4)
    finish(6)
    finish(8)

    turned()

    @pl.when(core == 0)
    def _():
        within_mirror(0).wait_recv()
        place(cross_ref.at[0, 0], 0, wide(summed[2, yh]) + wide(home_near[0, 0]))
        remote(home_near.at[1, 1], home_near.at[1, 1], home_s.at[2, 0], near_r.at[1, 1], mate).wait_recv()
        remote(home_near.at[2, 1], home_near.at[2, 1], home_s.at[2, 0], near_r.at[2, 1], mate).wait_recv()
        place(cross_ref.at[0, 0], 1, wide(home_near[1, 1]) + wide(home_near[2, 1]))

    mine = jnp.where(yl == 0, 3, 5)

    def gather_home(box, sems, first, out):
        for k in range(2):
            remote(box.at[0, k], box.at[0, k], home_s.at[0, 0], sems.at[0, k], mirror).wait_recv()
        for source in (1, 2):
            for h in range(2):
                remote(
                    box.at[source, h], box.at[source, h], home_s.at[0, 0], sems.at[source, h], mirror
                ).wait_recv()
        for k in range(2):
            place(
                out, k,
                wide(summed[first + k, yh]) + wide(box[0, k]) + wide(box[1, k]) + wide(box[2, k]),
            )

    gather_home(home_far, far_r, mine, cross_ref.at[0, 1])

    @pl.when(core == 1)
    def _():
        gather_home(home_near, near_r, 7, cross_ref.at[0, 0])

    score_home_copy().wait_recv()
    for k in range(2):
        scores = wide(score_sum[k]) + wide(score_home[k])
        place(score_ref, k, jnp.where(yh == 0, scores[0:4], scores[4:8]))

    score_home_copy().wait_send()
    next_copy().wait_send()

    @pl.when(yh == 0)
    def _():
        for xv in range(4):
            turn_copy(xv).wait_send()

    for side in range(2):
        score_hop_copy(side).wait_send()
        score_fold_copy(side).wait_send()
    for step in range(1, 8):
        ring_copy(step).wait_send()
    over_copy().wait_send()
    note_mate_copy().wait_send()
    mate_copy(0).wait_send()

    @pl.when(core == 0)
    def _():
        mate_copy(1).wait_send()

    for step in range(8):
        inner_copy(step).wait_send()
        along_copy(step).wait_send()
    for k in range(2):
        cross_copy(k).wait_send()
    for p in range(PIECES):
        for side in range(2):
            hop_copy(p, side).wait_send()
            for h in range(2):
                fold_copy(p, side, h).wait_send()
            home_op(p, side, lambda copy: copy.wait_send())


def gram_tiles(stored, acts, grads, in_rows, out_rows, classes):
    bf16 = jnp.bfloat16
    dma = pltpu.SemaphoreType.DMA
    return pl.pallas_call(
        tiles_kernel,
        out_shape=(
            jax.ShapeDtypeStruct((1, 128, 1024), bf16),
            jax.ShapeDtypeStruct((1, 2, 128, 1024), bf16),
            jax.ShapeDtypeStruct((4, 1024), bf16),
        ),
        in_specs=[pl.BlockSpec(memory_space=pl.ANY)] * 5 + [pl.BlockSpec(memory_space=pltpu.SMEM)],
        out_specs=(pl.BlockSpec(memory_space=pltpu.VMEM),) * 3,
        scratch_shapes=[
            pltpu.VMEM((14, 512, 1024), bf16),
            pltpu.VMEM((PIECES, 4, 2, 128, 512), bf16),
            pltpu.VMEM((PIECES, 2, 128, 512), bf16),
            pltpu.VMEM((PIECES, 2, 2, 128, 512), bf16),
            pltpu.VMEM((PIECES, 2, 128, 512), bf16),
            pltpu.VMEM((2, 128, 512), bf16),
            pltpu.VMEM((3, 2, 128, 512), bf16),
            pltpu.VMEM((3, 2, 128, 512), bf16),
            pltpu.VMEM((2, 128, 4096), bf16),
            pltpu.VMEM((2, 128, 4096), bf16),
            pltpu.VMEM((2, RANK, 4096), bf16),
            pltpu.VMEM((2, RANK, 4096), bf16),
            pltpu.VMEM((16, 384), jnp.float32),
            pltpu.VMEM((2, 8, 2, 16, 384), bf16),
            pltpu.VMEM((64, 2048), bf16),
            pltpu.VMEM((4, 2, 16, 512), bf16),
            pltpu.VMEM((2, 16, 512), bf16),
            pltpu.VMEM((2, 2, 16, 512), bf16),
            pltpu.VMEM((2, 16, 512), bf16),
            pltpu.VMEM((2, 16, 512), bf16),
            pltpu.VMEM((1024, 2, 1024), bf16),
            pltpu.VMEM((5, 128, 128), bf16),
            pltpu.VMEM((5, 128, 128), bf16),
            dma((5,)), dma((5,)),
            dma((4,)), dma((7,)), dma((7,)), dma((2,)), dma((2,)),
            dma((2,)), dma((2,)), dma((2,)), dma((2,)), dma, dma,
            dma((8,)), dma((2,)), dma((2,)), dma((8,)), dma((8,)), dma((8,)), dma((8,)), dma((2,)), dma((2,)),
            dma((PIECES, 2)), dma((PIECES, 2)), dma((PIECES, 2, 2)), dma((PIECES, 2, 2)), dma((PIECES, 2)),
            dma((2,)), dma((3, 2)), dma((3, 2)),
        ],
        compiler_params=pltpu.CompilerParams(
            collective_id=0, has_side_effects=True, vmem_limit_bytes=56 * 2**20
        ),
        cost_estimate=pl.CostEstimate(flops=13 * 10**9, bytes_accessed=8 * 2**20, transcendentals=0),
        name="gram_tiles",
    )(stored, acts, grads, in_rows, out_rows, classes)


def settle_kernel(*refs):
    for src, dst in zip(refs[0:3], refs[3:6]):
        dst[...] = src[...]


def settle(*results):
    return pl.pallas_call(
        settle_kernel,
        out_shape=tuple(jax.ShapeDtypeStruct(r.shape, r.dtype) for r in results),
        in_specs=[pl.BlockSpec(memory_space=pltpu.VMEM)] * 3,
        out_specs=(pl.BlockSpec(memory_space=pltpu.VMEM),) * 3,
        name="settle",
    )(*results)


def per_device(activations, out_grads, in_factor, out_factor, stored_rows, example_class):
    layer_count = activations.shape[0]
    model_width = activations.shape[3]
    return settle(*gram_tiles(
        stored_rows,
        activations.reshape(layer_count, -1, model_width),
        out_grads.reshape(layer_count, -1, model_width),
        in_factor.transpose(0, 2, 1),
        out_factor.transpose(0, 2, 1),
        example_class,
    ))


def solution(mesh):
    placed = (
        P("layer", "group", None, None),
        P("layer", "group", None, None),
        P("layer", None, None),
        P("layer", None, None),
        P("group", "layer", None),
        P("group"),
    )
    return jax.shard_map(
        per_device,
        mesh=mesh,
        in_specs=placed,
        out_specs=(P("group", "layer", None), P("group", None, "layer", None), P("layer", "group")),
        check_vma=False,
    )
```

```python
import functools

import jax
import jax.numpy as jnp
from jax import lax
from jax.experimental import pallas as pl
from jax.experimental.pallas import tpu as pltpu
from jax.sharding import PartitionSpec as P

RANK = 32
MESH = pl.DeviceIdType.MESH
OWN, MATE, INNER, ALONG, CROSS = 0, 4, 8, 10, 12
PIECES = 9


def inner_block(left_rows, right_rows):
    return lax.dot_general(
        left_rows, right_rows, (((1,), (1,)), ((), ())), preferred_element_type=jnp.float32
    )


def tiles_kernel(
    stored_hbm, acts_hbm, grads_hbm, in_hbm, out_hbm, class_ref, self_ref, cross_ref, score_ref,
    chunks, parts, hop, near_in, summed, home_self, home_near, home_far,
    acts, grads, in_rows, out_rows, note, notes, class_rows,
    score_parts, score_hop, score_near, score_sum, score_home,
    raw, turn_out, turn_in, turn_s, turn_r, load_sem, ring_s, ring_r, share_s, share_r, sc_hop_s, sc_hop_r, sc_fold_s, sc_fold_r, sc_home_s, sc_home_r,
    own_sem, mate_s, mate_r, inner_s, inner_r, along_s, along_r, cross_s, cross_r,
    hop_s, hop_r, fold_s, fold_r, home_s, self_r, near_r, far_r,
):
    layer = lax.axis_index("layer")
    group = lax.axis_index("group")
    x, yh = layer // 2, layer % 2
    z, yl, core = group // 4, (group // 2) % 2, group % 2
    other = 1 - yh

    def at(xx, hh, gg):
        return (lax.rem(xx + 4, 4) * 2 + hh, lax.rem(gg + 32, 32))

    right, left = at(x + 1, yh, group), at(x - 1, yh, group)
    mirror = at(x, other, group)
    mate = at(x, yh, group + 1 - 2 * core)
    across = at(x, yh, group + 2 - 4 * yl)
    onward = at(x, yh, group + 4 - 8 * yl)
    greeted = [right, left, mirror]
    for step in (1, -1, 2, -2):
        greeted += [at(x, yh, group + step), at(x, other, group + step)]
    greeted += [at(x, yh, group + 4 * step) for step in range(1, 8)]
    greeted += [at(x + step, other, group) for step in range(1, 4)]
    barrier = pltpu.get_barrier_semaphore()
    for who in greeted:
        pl.semaphore_signal(barrier, inc=1, device_id=who, device_id_type=MESH)
    own_copies = [
        pltpu.make_async_copy(stored_hbm.at[rows], raw.at[rows], own_sem.at[step])
        for step, rows in enumerate([pl.ds(256 * (step % 4) + 128 * (step // 4), 128) for step in range(8)])
    ]
    loads = [
        pltpu.make_async_copy(src, dst, load_sem.at[k])
        for k, (src, dst) in enumerate(
            [(acts_hbm, acts), (grads_hbm, grads), (in_hbm, in_rows), (out_hbm, out_rows)]
        )
    ]
    for copy in own_copies + loads:
        copy.start()
    pair = lax.broadcasted_iota(jnp.int32, (128, 256), 1)
    wanted_row = lax.broadcasted_iota(jnp.int32, (128, 256), 0) * 2
    pick = [(pair == wanted_row + f).astype(jnp.float32).astype(jnp.bfloat16) for f in range(2)]
    for copy in own_copies:
        copy.wait()

    def take_apart(step, carry):
        k, xv = step // 4, step % 4
        rows = raw[pl.ds(pl.multiple_of(256 * xv + 128 * k, 128), 128)].reshape(256, 1024)
        for f in range(2):
            chunks[OWN + 2 * k + f, pl.ds(pl.multiple_of(128 * xv, 128), 128), :] = jnp.dot(
                pick[f], rows, preferred_element_type=jnp.float32
            ).astype(jnp.bfloat16)
        return carry

    lax.fori_loop(0, 8, take_apart, 0)
    pl.semaphore_wait(barrier, len(greeted))

    def remote(src, dst, send, recv, who):
        return pltpu.make_async_remote_copy(
            src_ref=src, dst_ref=dst, send_sem=send, recv_sem=recv, device_id=who, device_id_type=MESH
        )

    def rows_of(step):
        return step // 4, pl.ds((step % 4) * 128, 128)

    def inner_copy(step):
        k, rows = rows_of(step)
        return remote(chunks.at[OWN + 2 * k + yl, rows], chunks.at[INNER + k, rows], inner_s.at[step], inner_r.at[step], across)

    def along_copy(step):
        k, rows = rows_of(step)
        return remote(
            chunks.at[INNER + k, rows], chunks.at[ALONG + k, rows], along_s.at[step], along_r.at[step], onward
        )

    def mate_copy(k):
        return remote(chunks.at[pl.ds(OWN + 2 * k, 2)], chunks.at[pl.ds(MATE + 2 * k, 2)], mate_s.at[k], mate_r.at[k], mate)

    passes_inner = yl == core
    passed = jnp.where(passes_inner, INNER, ALONG)

    def cross_copy(step):
        k, rows = rows_of(step)
        return remote(
            chunks.at[passed + k, rows], chunks.at[CROSS + k, rows], cross_s.at[step], cross_r.at[step], mate
        )

    def share(p, ref, h):
        if p == 0:
            return ref.at[h, :, pl.ds(0, 384)]
        if p == 1:
            return ref.at[0, :, pl.ds(256 * h, 256)]
        return ref.at[h]

    def hop_copy(p, side):
        return remote(
            share(p, parts.at[p, lax.rem(x + 2, 4)], side), share(p, hop.at[p], side),
            hop_s.at[p, side], hop_r.at[p, side], right if side == 0 else left,
        )

    def fold_copy(p, side, h):
        to = lax.rem(x + 1, 4) if side == 0 else lax.rem(x + 3, 4)
        return remote(
            share(p, parts.at[p, to], h), share(p, near_in.at[p, side], h),
            fold_s.at[p, side, h], fold_r.at[p, side, h], right if side == 0 else left,
        )

    for step in range(4):
        inner_copy(step).start()
    mate_copy(0).start()

    @pl.when(core == 0)
    def _():
        mate_copy(1).start()

    def send_share(p, h):
        hop_copy(p, h).start()
        fold_copy(p, 1 - h, h).start()

    def product(lefts, rights, cols):
        total = None
        for a, b in zip(lefts, rights):
            term = inner_block(chunks[a], chunks[b, cols, :])
            total = term if total is None else total + term
        return total.astype(jnp.bfloat16).reshape(4, 128, 256)

    def diagonal():
        for i in range(2):
            slots = [OWN + 2 * i, OWN + 2 * i + 1]
            for n in range(2):
                total = product(slots, slots, pl.ds(256 * n, 256))
                for xu in range(4):
                    for xv in (2 * n, 2 * n + 1):
                        d = (xv - xu) % 4
                        if d < 3:
                            parts[0, xu, i, :, 128 * d : 128 * d + 128] = total[
                                xu, :, 128 * (xv - 2 * n) : 128 * (xv - 2 * n) + 128
                            ]
            send_share(0, i)

    def compute(p, left_slots, right_slots):
        for i in range(1 if p == 1 else 2):
            lefts, rights = left_slots(i), right_slots(i)

            def columns(n, carry):
                cols = pl.ds(pl.multiple_of(n * 256, 256), 256)
                parts[p, :, i, :, cols] = product(lefts, rights, cols)
                return carry

            lax.fori_loop(0, 2, columns, 0)
            send_share(p, i)
            if p == 1:
                send_share(p, 1)

    half = 1 - yl

    def half_piece(p, slot, is_row):
        def lefts(i):
            return [jnp.where(is_row, slot, OWN + 2 * i + half)]

        def rights(i):
            return [jnp.where(is_row, OWN + 2 * i + half, slot)]

        compute(p, lefts, rights)

    def fold(p):
        for side in range(2):
            to = lax.rem(x + 1, 4) if side == 0 else lax.rem(x + 3, 4)
            hop_copy(p, side).wait_recv()
            mine, come = share(p, parts.at[p, to], side), share(p, hop.at[p], side)
            mine[...] = (mine[...].astype(jnp.float32) + come[...].astype(jnp.float32)).astype(jnp.bfloat16)
            fold_copy(p, side, side).start()

    def total_of(p, h):
        for side in range(2):
            fold_copy(p, side, h).wait_recv()
        share(p, summed.at[p], h)[...] = (
            share(p, parts.at[p, x], h)[...].astype(jnp.float32)
            + share(p, near_in.at[p, 0], h)[...].astype(jnp.float32)
            + share(p, near_in.at[p, 1], h)[...].astype(jnp.float32)
        ).astype(jnp.bfloat16)

    def diagonal_home(h):
        return remote(share(0, summed.at[0], h), home_self.at[0, :, pl.ds(0, 384)], home_s.at[0, h], self_r.at[0], mirror)

    def beside_home():
        return remote(summed.at[1, 0], home_self.at[1], home_s.at[1, 0], self_r.at[1], mirror)

    def turn_copy(xv):
        return remote(turn_out.at[xv], turn_in.at[x], turn_s.at[xv], turn_r.at[x], at(xv, 1, group))

    def next_copy():
        return remote(turn_out.at[4], turn_in.at[4], turn_s.at[4], turn_r.at[4], right)

    def within_mirror(h):
        return remote(summed.at[2, h], home_near.at[0, 0], home_s.at[2, h], near_r.at[0, 0], mirror)

    def within_mate(h):
        return remote(summed.at[2, h], home_near.at[1, 1], home_s.at[2, h], near_r.at[1, 1], mate)

    def within_mate_mirror(h):
        return remote(
            summed.at[2, h], home_near.at[2, 1], home_s.at[2, h], near_r.at[2, 1],
            at(x, other, group + 1 - 2 * core),
        )

    def col_home(p, k, h, box, sems):
        return remote(summed.at[p, h], box.at[0, k], home_s.at[p, h], sems.at[0, k], mirror)

    def row_home(p, k, h, box, sems, back):
        place = jnp.where(yh == k, 1, 2)
        return remote(
            summed.at[p, h], box.at[place, h], home_s.at[p, h], sems.at[place, h], at(x, k, group - back)
        )

    def home_op(p, h, op):
        if p == 0:

            @pl.when(other == h)
            def _():
                op(diagonal_home(h))
        elif p == 1:
            if h == 1:

                @pl.when(yh == 1)
                def _():
                    op(beside_home())
        elif p == 2:

            @pl.when((core == 0) & (other == h))
            def _():
                op(within_mirror(h))

            @pl.when((core == 1) & (yh == h))
            def _():
                op(within_mate(h))

            @pl.when((core == 1) & (other == h))
            def _():
                op(within_mate_mirror(h))
        else:
            k = (p - 3) % 2
            is_row = {0: yl == 1, 1: yl == 0, 2: core == 0}[(p - 3) // 2]
            box, sems, back = (home_far, far_r, 2) if p < 7 else (home_near, near_r, 1)

            @pl.when(is_row)
            def _():
                op(row_home(p, k, h, box, sems, back))

            @pl.when(jnp.logical_not(is_row) & (other == h))
            def _():
                op(col_home(p, k, h, box, sems))

    def finish(p):
        for h in range(2):
            total_of(p, h)
            home_op(p, h, lambda copy: copy.start())

    def pass_on(step):
        inner_copy(step).wait_recv()
        along_copy(step).start()
        if step < 4:
            inner_copy(step + 4).start()

        @pl.when(passes_inner)
        def _():
            cross_copy(step).start()

    def take_along(k):
        for step in range(4 * k, 4 * k + 4):
            along_copy(step).wait_recv()

            @pl.when(jnp.logical_not(passes_inner))
            def _():
                cross_copy(step).start()

    def piece_inner(k):
        half_piece(3 + k, INNER + k, yl == 1)

    def piece_along(k):
        half_piece(5 + k, ALONG + k, yl == 0)

    def piece_cross(k):
        for step in range(4 * k, 4 * k + 4):
            cross_copy(step).wait_recv()
        half_piece(7 + k, CROSS + k, core == 0)

    def over_copy():
        return remote(notes.at[0, 0, 0], notes.at[0, 0, 1], share_s.at[0], share_r.at[0], across)

    def ring_copy(step):
        return remote(
            notes.at[0, 0], notes.at[0, step], ring_s.at[step - 1], ring_r.at[step - 1],
            at(x, yh, group + 4 * step),
        )

    def note_mate_copy():
        return remote(notes.at[0], notes.at[1], share_s.at[1], share_r.at[1], mate)

    def exact_spread(value, spread):
        total = None
        for _ in range(3):
            part = value.astype(jnp.bfloat16)
            value = value - part.astype(jnp.float32)
            term = jnp.dot(part, spread, preferred_element_type=jnp.float32)
            total = term if total is None else total + term
        return total

    def project():
        for copy in loads:
            copy.wait()
        feature = lax.broadcasted_iota(jnp.int32, (RANK, RANK * RANK), 1)
        factor = lax.broadcasted_iota(jnp.int32, (RANK, RANK * RANK), 0)
        to_p = (feature // RANK == factor).astype(jnp.float32).astype(jnp.bfloat16)
        to_q = (feature % RANK == factor).astype(jnp.float32).astype(jnp.bfloat16)
        for k in range(2):
            left_side = exact_spread(inner_block(acts[k], in_rows[k]), to_p)
            right_side = exact_spread(inner_block(grads[k], out_rows[k]), to_q)
            outer = left_side * right_side
            for e in range(2):
                fresh = jnp.sum(outer[64 * e : 64 * e + 64], axis=0, keepdims=True)
                for c in range(4):
                    row = 8 * e + 4 * k + c
                    note[row : row + 1, 0:256] = fresh[:, 256 * c : 256 * c + 256]
        for e in range(2):
            note[8 * e : 8 * e + 8, 256:384] = jnp.full((8, 128), class_ref[e], jnp.int32).astype(jnp.float32)
        notes[0, 0, 0] = note[...].astype(jnp.bfloat16)
        over_copy().start()

    def share_first():
        over_copy().wait_recv()
        for step in range(1, 8):
            ring_copy(step).start()

    def share_second():
        for step in range(1, 8):
            ring_copy(step).wait_recv()
        note_mate_copy().start()

    def score_hop_copy(side):
        return remote(
            score_parts.at[lax.rem(x + 2, 4), side], score_hop.at[side], sc_hop_s.at[side], sc_hop_r.at[side],
            right if side == 0 else left,
        )

    def score_fold_copy(side):
        to = lax.rem(x + 1, 4) if side == 0 else lax.rem(x + 3, 4)
        return remote(
            score_parts.at[to], score_near.at[side], sc_fold_s.at[side], sc_fold_r.at[side],
            right if side == 0 else left,
        )

    def score_home_copy():
        return remote(score_sum, score_home, sc_home_s, sc_home_r, mirror)

    def score_compute():
        note_mate_copy().wait_recv()
        rows = notes[...].reshape(512, 384)
        fresh = rows[:, 0:256]
        classes = rows[:, 256:384].astype(jnp.float32).T[0:64]
        spot = lax.broadcasted_iota(jnp.int32, (64, 512), 0)
        wanted = jnp.where(spot % 16 < 8, spot // 16 * 8 + spot % 16, -1).astype(jnp.float32)
        column = lax.broadcasted_iota(jnp.int32, (64, 512), 1) % 8
        for c in range(8):
            picked = jnp.where((classes == wanted) & (column == c), 1.0, 0.0).astype(jnp.bfloat16)
            class_rows[:, 256 * c : 256 * c + 256] = jnp.dot(
                picked, fresh, preferred_element_type=jnp.float32
            ).astype(jnp.bfloat16)
        for k in range(2):
            part = inner_block(class_rows[:, 0:1024], chunks[OWN + 2 * k]) + inner_block(
                class_rows[:, 1024:2048], chunks[OWN + 2 * k + 1]
            )
            score_parts[:, k] = part.astype(jnp.bfloat16).reshape(4, 16, 512)
        for side in range(2):
            score_hop_copy(side).start()

    def score_fold():
        for side in range(2):
            to = lax.rem(x + 1, 4) if side == 0 else lax.rem(x + 3, 4)
            score_hop_copy(side).wait_recv()
            score_parts[to, side] = (
                score_parts[to, side].astype(jnp.float32) + score_hop[side].astype(jnp.float32)
            ).astype(jnp.bfloat16)
            score_fold_copy(side).start()

    def score_finish():
        for side in range(2):
            score_fold_copy(side).wait_recv()
        score_sum[...] = (
            score_parts[x].astype(jnp.float32)
            + score_near[0].astype(jnp.float32)
            + score_near[1].astype(jnp.float32)
        ).astype(jnp.bfloat16)
        score_home_copy().start()

    def place(ref, k, value):
        for xv in range(4):
            ref[:, pl.ds(256 * xv + 128 * k, 128)] = value[:, 128 * xv : 128 * xv + 128].astype(jnp.bfloat16)

    def wide(value):
        return value.astype(jnp.float32)

    def column(xv, k):
        return pl.ds(pl.multiple_of(256 * xv + 128 * k, 128), 128)

    def turn():
        remote(home_self.at[0, :, pl.ds(0, 384)], home_self.at[0, :, pl.ds(0, 384)], home_s.at[0, 0], self_r.at[0], mirror).wait_recv()
        diag = (wide(summed[0, yh, :, 0:384]) + wide(home_self[0, :, 0:384])).astype(jnp.bfloat16)
        for d in range(3):
            self_ref[0, :, column(lax.rem(x + d, 4), yh)] = diag[:, 128 * d : 128 * d + 128]
        turn_out[4] = diag[:, 128:256]
        next_copy().start()

        @pl.when(yh == 0)
        def _():
            beside_home().wait_recv()
            final = wide(summed[1, 0]) + wide(home_self[1])
            place(self_ref.at[0], 1, final)
            for xv in range(4):
                turn_out[xv] = final[:, 128 * xv : 128 * xv + 128].astype(jnp.bfloat16)
                turn_copy(xv).start()

    def turned():
        next_copy().wait_recv()
        self_ref[0, :, column(lax.rem(x + 3, 4), yh)] = wide(turn_in[4]).T.astype(jnp.bfloat16)

        @pl.when(yh == 1)
        def _():
            for xv in range(4):
                remote(turn_in.at[xv], turn_in.at[xv], turn_s.at[xv], turn_r.at[xv], mirror).wait_recv()
                self_ref[0, :, pl.ds(256 * xv, 128)] = wide(turn_in[xv]).T.astype(jnp.bfloat16)

    diagonal()
    compute(1, lambda i: [OWN, OWN + 1], lambda i: [OWN + 2, OWN + 3])
    project()
    pass_on(0)
    fold(0)
    mate_copy(0).wait_recv()

    @pl.when(core == 1)
    def _():
        mate_copy(1).wait_recv()

    theirs = jnp.where(core == 0, MATE, OWN + 2)
    compute(
        2,
        lambda i: [MATE * core + 2 * i, MATE * core + 2 * i + 1],
        lambda i: [theirs, theirs + 1],
    )
    fold(1)
    pass_on(1)
    fold(2)
    pass_on(2)
    pass_on(3)
    piece_inner(0)
    share_first()
    pass_on(4)
    take_along(0)
    piece_along(0)
    fold(3)
    piece_cross(0)
    fold(5)
    pass_on(5)
    fold(7)
    pass_on(6)
    share_second()
    pass_on(7)
    piece_inner(1)
    score_compute()
    finish(0)
    finish(1)
    finish(2)
    take_along(1)
    piece_along(1)
    finish(3)
    fold(4)
    score_fold()
    piece_cross(1)
    finish(5)
    finish(7)
    finish(4)
    fold(6)
    turn()
    score_finish()
    fold(8)
    finish(6)
    finish(8)

    turned()

    @pl.when(core == 0)
    def _():
        within_mirror(0).wait_recv()
        place(cross_ref.at[0, 0], 0, wide(summed[2, yh]) + wide(home_near[0, 0]))
        remote(home_near.at[1, 1], home_near.at[1, 1], home_s.at[2, 0], near_r.at[1, 1], mate).wait_recv()
        remote(home_near.at[2, 1], home_near.at[2, 1], home_s.at[2, 0], near_r.at[2, 1], mate).wait_recv()
        place(cross_ref.at[0, 0], 1, wide(home_near[1, 1]) + wide(home_near[2, 1]))

    mine = jnp.where(yl == 0, 3, 5)

    def gather_home(box, sems, first, out):
        for k in range(2):
            remote(box.at[0, k], box.at[0, k], home_s.at[0, 0], sems.at[0, k], mirror).wait_recv()
        for source in (1, 2):
            for h in range(2):
                remote(
                    box.at[source, h], box.at[source, h], home_s.at[0, 0], sems.at[source, h], mirror
                ).wait_recv()
        for k in range(2):
            place(
                out, k,
                wide(summed[first + k, yh]) + wide(box[0, k]) + wide(box[1, k]) + wide(box[2, k]),
            )

    gather_home(home_far, far_r, mine, cross_ref.at[0, 1])

    @pl.when(core == 1)
    def _():
        gather_home(home_near, near_r, 7, cross_ref.at[0, 0])

    score_home_copy().wait_recv()
    for k in range(2):
        scores = wide(score_sum[k]) + wide(score_home[k])
        place(score_ref, k, jnp.where(yh == 0, scores[0:4], scores[4:8]))

    score_home_copy().wait_send()
    next_copy().wait_send()

    @pl.when(yh == 0)
    def _():
        for xv in range(4):
            turn_copy(xv).wait_send()

    for side in range(2):
        score_hop_copy(side).wait_send()
        score_fold_copy(side).wait_send()
    for step in range(1, 8):
        ring_copy(step).wait_send()
    over_copy().wait_send()
    note_mate_copy().wait_send()
    mate_copy(0).wait_send()

    @pl.when(core == 0)
    def _():
        mate_copy(1).wait_send()

    for step in range(8):
        inner_copy(step).wait_send()
        along_copy(step).wait_send()
    for step in range(8):
        cross_copy(step).wait_send()
    for p in range(PIECES):
        for side in range(2):
            hop_copy(p, side).wait_send()
            for h in range(2):
                fold_copy(p, side, h).wait_send()
            home_op(p, side, lambda copy: copy.wait_send())


def gram_tiles(stored, acts, grads, in_rows, out_rows, classes):
    bf16 = jnp.bfloat16
    dma = pltpu.SemaphoreType.DMA
    return pl.pallas_call(
        tiles_kernel,
        out_shape=(
            jax.ShapeDtypeStruct((1, 128, 1024), bf16),
            jax.ShapeDtypeStruct((1, 2, 128, 1024), bf16),
            jax.ShapeDtypeStruct((4, 1024), bf16),
        ),
        in_specs=[pl.BlockSpec(memory_space=pl.ANY)] * 5 + [pl.BlockSpec(memory_space=pltpu.SMEM)],
        out_specs=(pl.BlockSpec(memory_space=pltpu.VMEM),) * 3,
        scratch_shapes=[
            pltpu.VMEM((14, 512, 1024), bf16),
            pltpu.VMEM((PIECES, 4, 2, 128, 512), bf16),
            pltpu.VMEM((PIECES, 2, 128, 512), bf16),
            pltpu.VMEM((PIECES, 2, 2, 128, 512), bf16),
            pltpu.VMEM((PIECES, 2, 128, 512), bf16),
            pltpu.VMEM((2, 128, 512), bf16),
            pltpu.VMEM((3, 2, 128, 512), bf16),
            pltpu.VMEM((3, 2, 128, 512), bf16),
            pltpu.VMEM((2, 128, 4096), bf16),
            pltpu.VMEM((2, 128, 4096), bf16),
            pltpu.VMEM((2, RANK, 4096), bf16),
            pltpu.VMEM((2, RANK, 4096), bf16),
            pltpu.VMEM((16, 384), jnp.float32),
            pltpu.VMEM((2, 8, 2, 16, 384), bf16),
            pltpu.VMEM((64, 2048), bf16),
            pltpu.VMEM((4, 2, 16, 512), bf16),
            pltpu.VMEM((2, 16, 512), bf16),
            pltpu.VMEM((2, 2, 16, 512), bf16),
            pltpu.VMEM((2, 16, 512), bf16),
            pltpu.VMEM((2, 16, 512), bf16),
            pltpu.VMEM((1024, 2, 1024), bf16),
            pltpu.VMEM((5, 128, 128), bf16),
            pltpu.VMEM((5, 128, 128), bf16),
            dma((5,)), dma((5,)),
            dma((4,)), dma((7,)), dma((7,)), dma((2,)), dma((2,)),
            dma((2,)), dma((2,)), dma((2,)), dma((2,)), dma, dma,
            dma((8,)), dma((2,)), dma((2,)), dma((8,)), dma((8,)), dma((8,)), dma((8,)), dma((8,)), dma((8,)),
            dma((PIECES, 2)), dma((PIECES, 2)), dma((PIECES, 2, 2)), dma((PIECES, 2, 2)), dma((PIECES, 2)),
            dma((2,)), dma((3, 2)), dma((3, 2)),
        ],
        compiler_params=pltpu.CompilerParams(
            collective_id=0, has_side_effects=True, vmem_limit_bytes=56 * 2**20
        ),
        cost_estimate=pl.CostEstimate(flops=13 * 10**9, bytes_accessed=8 * 2**20, transcendentals=0),
        name="gram_tiles",
    )(stored, acts, grads, in_rows, out_rows, classes)


def settle_kernel(*refs):
    for src, dst in zip(refs[0:3], refs[3:6]):
        dst[...] = src[...]


def settle(*results):
    return pl.pallas_call(
        settle_kernel,
        out_shape=tuple(jax.ShapeDtypeStruct(r.shape, r.dtype) for r in results),
        in_specs=[pl.BlockSpec(memory_space=pltpu.VMEM)] * 3,
        out_specs=(pl.BlockSpec(memory_space=pltpu.VMEM),) * 3,
        name="settle",
    )(*results)


def per_device(activations, out_grads, in_factor, out_factor, stored_rows, example_class):
    layer_count = activations.shape[0]
    model_width = activations.shape[3]
    return settle(*gram_tiles(
        stored_rows,
        activations.reshape(layer_count, -1, model_width),
        out_grads.reshape(layer_count, -1, model_width),
        in_factor.transpose(0, 2, 1),
        out_factor.transpose(0, 2, 1),
        example_class,
    ))


def solution(mesh):
    placed = (
        P("layer", "group", None, None),
        P("layer", "group", None, None),
        P("layer", None, None),
        P("layer", None, None),
        P("group", "layer", None),
        P("group"),
    )
    return jax.shard_map(
        per_device,
        mesh=mesh,
        in_specs=placed,
        out_specs=(P("group", "layer", None), P("group", None, "layer", None), P("layer", "group")),
        check_vma=False,
    )
```

```python
import functools

import jax
import jax.numpy as jnp
from jax import lax
from jax.experimental import pallas as pl
from jax.experimental.pallas import tpu as pltpu
from jax.sharding import PartitionSpec as P

RANK = 32
MESH = pl.DeviceIdType.MESH
OWN, MATE, INNER, ALONG, CROSS = 0, 4, 8, 10, 12
PIECES = 9


def inner_block(left_rows, right_rows):
    return lax.dot_general(
        left_rows, right_rows, (((1,), (1,)), ((), ())), preferred_element_type=jnp.float32
    )


def tiles_kernel(
    stored_hbm, acts_hbm, grads_hbm, in_hbm, out_hbm, class_ref, self_ref, cross_ref, score_ref,
    chunks, parts, hop, near_in, summed, home_self, home_near, home_far,
    acts, grads, in_rows, out_rows, note, notes, class_rows,
    score_parts, score_hop, score_near, score_sum, score_home,
    raw, turn_out, turn_in, turn_s, turn_r, load_sem, ring_s, ring_r, share_s, share_r, sc_hop_s, sc_hop_r, sc_fold_s, sc_fold_r, sc_home_s, sc_home_r,
    own_sem, mate_s, mate_r, inner_s, inner_r, along_s, along_r, cross_s, cross_r,
    hop_s, hop_r, fold_s, fold_r, home_s, self_r, near_r, far_r,
):
    layer = lax.axis_index("layer")
    group = lax.axis_index("group")
    x, yh = layer // 2, layer % 2
    z, yl, core = group // 4, (group // 2) % 2, group % 2
    other = 1 - yh

    def at(xx, hh, gg):
        return (lax.rem(xx + 4, 4) * 2 + hh, lax.rem(gg + 32, 32))

    right, left = at(x + 1, yh, group), at(x - 1, yh, group)
    mirror = at(x, other, group)
    mate = at(x, yh, group + 1 - 2 * core)
    across = at(x, yh, group + 2 - 4 * yl)
    onward = at(x, yh, group + 4 - 8 * yl)
    greeted = [right, left, mirror]
    for step in (1, -1, 2, -2):
        greeted += [at(x, yh, group + step), at(x, other, group + step)]
    greeted += [at(x, yh, group + 4 * step) for step in range(1, 8)]
    greeted += [at(x + step, other, group) for step in range(1, 4)]
    barrier = pltpu.get_barrier_semaphore()
    for who in greeted:
        pl.semaphore_signal(barrier, inc=1, device_id=who, device_id_type=MESH)
    own_copies = [
        pltpu.make_async_copy(stored_hbm.at[rows], raw.at[rows], own_sem.at[step])
        for step, rows in enumerate([pl.ds(256 * (step % 4) + 128 * (step // 4), 128) for step in range(8)])
    ]
    loads = [
        pltpu.make_async_copy(src, dst, load_sem.at[k])
        for k, (src, dst) in enumerate(
            [(acts_hbm, acts), (grads_hbm, grads), (in_hbm, in_rows), (out_hbm, out_rows)]
        )
    ]
    for copy in own_copies + loads:
        copy.start()
    pair = lax.broadcasted_iota(jnp.int32, (128, 256), 1)
    wanted_row = lax.broadcasted_iota(jnp.int32, (128, 256), 0) * 2
    pick = [(pair == wanted_row + f).astype(jnp.float32).astype(jnp.bfloat16) for f in range(2)]
    for copy in own_copies:
        copy.wait()

    def take_apart(step, carry):
        k, xv = step // 4, step % 4
        rows = raw[pl.ds(pl.multiple_of(256 * xv + 128 * k, 128), 128)].reshape(256, 1024)
        for f in range(2):
            chunks[OWN + 2 * k + f, pl.ds(pl.multiple_of(128 * xv, 128), 128), :] = jnp.dot(
                pick[f], rows, preferred_element_type=jnp.float32
            ).astype(jnp.bfloat16)
        return carry

    lax.fori_loop(0, 8, take_apart, 0)
    pl.semaphore_wait(barrier, len(greeted))

    def remote(src, dst, send, recv, who):
        return pltpu.make_async_remote_copy(
            src_ref=src, dst_ref=dst, send_sem=send, recv_sem=recv, device_id=who, device_id_type=MESH
        )

    def rows_of(step):
        return step // 4, pl.ds((step % 4) * 128, 128)

    def inner_copy(step):
        k, rows = rows_of(step)
        return remote(chunks.at[OWN + 2 * k + yl, rows], chunks.at[INNER + k, rows], inner_s.at[step], inner_r.at[step], across)

    def along_copy(step):
        k, rows = rows_of(step)
        return remote(
            chunks.at[INNER + k, rows], chunks.at[ALONG + k, rows], along_s.at[step], along_r.at[step], onward
        )

    def mate_copy(k):
        return remote(chunks.at[pl.ds(OWN + 2 * k, 2)], chunks.at[pl.ds(MATE + 2 * k, 2)], mate_s.at[k], mate_r.at[k], mate)

    passes_inner = yl == core
    passed = jnp.where(passes_inner, INNER, ALONG)

    def cross_copy(step):
        k, rows = rows_of(step)
        return remote(
            chunks.at[passed + k, rows], chunks.at[CROSS + k, rows], cross_s.at[step], cross_r.at[step], mate
        )

    def share(p, ref, h):
        if p == 0:
            return ref.at[h, :, pl.ds(0, 384)]
        if p == 1:
            return ref.at[0, :, pl.ds(256 * h, 256)]
        return ref.at[h]

    def hop_copy(p, side):
        return remote(
            share(p, parts.at[p, lax.rem(x + 2, 4)], side), share(p, hop.at[p], side),
            hop_s.at[p, side], hop_r.at[p, side], right if side == 0 else left,
        )

    def fold_copy(p, side, h):
        to = lax.rem(x + 1, 4) if side == 0 else lax.rem(x + 3, 4)
        return remote(
            share(p, parts.at[p, to], h), share(p, near_in.at[p, side], h),
            fold_s.at[p, side, h], fold_r.at[p, side, h], right if side == 0 else left,
        )

    for step in range(3):
        inner_copy(step).start()
    mate_copy(0).start()

    @pl.when(core == 0)
    def _():
        mate_copy(1).start()

    def send_share(p, h):
        hop_copy(p, h).start()
        fold_copy(p, 1 - h, h).start()

    def product(lefts, rights, cols):
        total = None
        for a, b in zip(lefts, rights):
            term = inner_block(chunks[a], chunks[b, cols, :])
            total = term if total is None else total + term
        return total.astype(jnp.bfloat16).reshape(4, 128, 256)

    def diagonal():
        for i in range(2):
            slots = [OWN + 2 * i, OWN + 2 * i + 1]
            for n in range(2):
                total = product(slots, slots, pl.ds(256 * n, 256))
                for xu in range(4):
                    for xv in (2 * n, 2 * n + 1):
                        d = (xv - xu) % 4
                        if d < 3:
                            parts[0, xu, i, :, 128 * d : 128 * d + 128] = total[
                                xu, :, 128 * (xv - 2 * n) : 128 * (xv - 2 * n) + 128
                            ]
            send_share(0, i)

    def compute(p, left_slots, right_slots):
        for i in range(1 if p == 1 else 2):
            lefts, rights = left_slots(i), right_slots(i)

            def columns(n, carry):
                cols = pl.ds(pl.multiple_of(n * 256, 256), 256)
                parts[p, :, i, :, cols] = product(lefts, rights, cols)
                return carry

            lax.fori_loop(0, 2, columns, 0)
            send_share(p, i)
            if p == 1:
                send_share(p, 1)

    half = 1 - yl

    def half_piece(p, slot, is_row):
        def lefts(i):
            return [jnp.where(is_row, slot, OWN + 2 * i + half)]

        def rights(i):
            return [jnp.where(is_row, OWN + 2 * i + half, slot)]

        compute(p, lefts, rights)

    def fold(p):
        for side in range(2):
            to = lax.rem(x + 1, 4) if side == 0 else lax.rem(x + 3, 4)
            hop_copy(p, side).wait_recv()
            mine, come = share(p, parts.at[p, to], side), share(p, hop.at[p], side)
            mine[...] = (mine[...].astype(jnp.float32) + come[...].astype(jnp.float32)).astype(jnp.bfloat16)
            fold_copy(p, side, side).start()

    def total_of(p, h):
        for side in range(2):
            fold_copy(p, side, h).wait_recv()
        share(p, summed.at[p], h)[...] = (
            share(p, parts.at[p, x], h)[...].astype(jnp.float32)
            + share(p, near_in.at[p, 0], h)[...].astype(jnp.float32)
            + share(p, near_in.at[p, 1], h)[...].astype(jnp.float32)
        ).astype(jnp.bfloat16)

    def diagonal_home(h):
        return remote(share(0, summed.at[0], h), home_self.at[0, :, pl.ds(0, 384)], home_s.at[0, h], self_r.at[0], mirror)

    def beside_home():
        return remote(summed.at[1, 0], home_self.at[1], home_s.at[1, 0], self_r.at[1], mirror)

    def turn_copy(xv):
        return remote(turn_out.at[xv], turn_in.at[x], turn_s.at[xv], turn_r.at[x], at(xv, 1, group))

    def next_copy():
        return remote(turn_out.at[4], turn_in.at[4], turn_s.at[4], turn_r.at[4], right)

    def within_mirror(h):
        return remote(summed.at[2, h], home_near.at[0, 0], home_s.at[2, h], near_r.at[0, 0], mirror)

    def within_mate(h):
        return remote(summed.at[2, h], home_near.at[1, 1], home_s.at[2, h], near_r.at[1, 1], mate)

    def within_mate_mirror(h):
        return remote(
            summed.at[2, h], home_near.at[2, 1], home_s.at[2, h], near_r.at[2, 1],
            at(x, other, group + 1 - 2 * core),
        )

    def col_home(p, k, h, box, sems):
        return remote(summed.at[p, h], box.at[0, k], home_s.at[p, h], sems.at[0, k], mirror)

    def row_home(p, k, h, box, sems, back):
        place = jnp.where(yh == k, 1, 2)
        return remote(
            summed.at[p, h], box.at[place, h], home_s.at[p, h], sems.at[place, h], at(x, k, group - back)
        )

    def home_op(p, h, op):
        if p == 0:

            @pl.when(other == h)
            def _():
                op(diagonal_home(h))
        elif p == 1:
            if h == 1:

                @pl.when(yh == 1)
                def _():
                    op(beside_home())
        elif p == 2:

            @pl.when((core == 0) & (other == h))
            def _():
                op(within_mirror(h))

            @pl.when((core == 1) & (yh == h))
            def _():
                op(within_mate(h))

            @pl.when((core == 1) & (other == h))
            def _():
                op(within_mate_mirror(h))
        else:
            k = (p - 3) % 2
            is_row = {0: yl == 1, 1: yl == 0, 2: core == 0}[(p - 3) // 2]
            box, sems, back = (home_far, far_r, 2) if p < 7 else (home_near, near_r, 1)

            @pl.when(is_row)
            def _():
                op(row_home(p, k, h, box, sems, back))

            @pl.when(jnp.logical_not(is_row) & (other == h))
            def _():
                op(col_home(p, k, h, box, sems))

    def finish(p):
        for h in range(2):
            total_of(p, h)
            home_op(p, h, lambda copy: copy.start())

    def pass_on(step):
        inner_copy(step).wait_recv()
        along_copy(step).start()
        if step < 5:
            inner_copy(step + 3).start()

        @pl.when(passes_inner)
        def _():
            cross_copy(step).start()

    def take_along(k):
        for step in range(4 * k, 4 * k + 4):
            along_copy(step).wait_recv()

            @pl.when(jnp.logical_not(passes_inner))
            def _():
                cross_copy(step).start()

    def piece_inner(k):
        half_piece(3 + k, INNER + k, yl == 1)

    def piece_along(k):
        half_piece(5 + k, ALONG + k, yl == 0)

    def piece_cross(k):
        for step in range(4 * k, 4 * k + 4):
            cross_copy(step).wait_recv()
        half_piece(7 + k, CROSS + k, core == 0)

    def over_copy():
        return remote(notes.at[0, 0, 0], notes.at[0, 0, 1], share_s.at[0], share_r.at[0], across)

    def ring_copy(step):
        return remote(
            notes.at[0, 0], notes.at[0, step], ring_s.at[step - 1], ring_r.at[step - 1],
            at(x, yh, group + 4 * step),
        )

    def note_mate_copy():
        return remote(notes.at[0], notes.at[1], share_s.at[1], share_r.at[1], mate)

    def exact_spread(value, spread):
        total = None
        for _ in range(3):
            part = value.astype(jnp.bfloat16)
            value = value - part.astype(jnp.float32)
            term = jnp.dot(part, spread, preferred_element_type=jnp.float32)
            total = term if total is None else total + term
        return total

    def project():
        for copy in loads:
            copy.wait()
        feature = lax.broadcasted_iota(jnp.int32, (RANK, RANK * RANK), 1)
        factor = lax.broadcasted_iota(jnp.int32, (RANK, RANK * RANK), 0)
        to_p = (feature // RANK == factor).astype(jnp.float32).astype(jnp.bfloat16)
        to_q = (feature % RANK == factor).astype(jnp.float32).astype(jnp.bfloat16)
        for k in range(2):
            left_side = exact_spread(inner_block(acts[k], in_rows[k]), to_p)
            right_side = exact_spread(inner_block(grads[k], out_rows[k]), to_q)
            outer = left_side * right_side
            for e in range(2):
                fresh = jnp.sum(outer[64 * e : 64 * e + 64], axis=0, keepdims=True)
                for c in range(4):
                    row = 8 * e + 4 * k + c
                    note[row : row + 1, 0:256] = fresh[:, 256 * c : 256 * c + 256]
        for e in range(2):
            note[8 * e : 8 * e + 8, 256:384] = jnp.full((8, 128), class_ref[e], jnp.int32).astype(jnp.float32)
        notes[0, 0, 0] = note[...].astype(jnp.bfloat16)
        over_copy().start()

    def share_first():
        over_copy().wait_recv()
        for step in range(1, 8):
            ring_copy(step).start()

    def share_second():
        for step in range(1, 8):
            ring_copy(step).wait_recv()
        note_mate_copy().start()

    def score_hop_copy(side):
        return remote(
            score_parts.at[lax.rem(x + 2, 4), side], score_hop.at[side], sc_hop_s.at[side], sc_hop_r.at[side],
            right if side == 0 else left,
        )

    def score_fold_copy(side):
        to = lax.rem(x + 1, 4) if side == 0 else lax.rem(x + 3, 4)
        return remote(
            score_parts.at[to], score_near.at[side], sc_fold_s.at[side], sc_fold_r.at[side],
            right if side == 0 else left,
        )

    def score_home_copy():
        return remote(score_sum, score_home, sc_home_s, sc_home_r, mirror)

    def score_compute():
        note_mate_copy().wait_recv()
        rows = notes[...].reshape(512, 384)
        fresh = rows[:, 0:256]
        classes = rows[:, 256:384].astype(jnp.float32).T[0:64]
        spot = lax.broadcasted_iota(jnp.int32, (64, 512), 0)
        wanted = jnp.where(spot % 16 < 8, spot // 16 * 8 + spot % 16, -1).astype(jnp.float32)
        column = lax.broadcasted_iota(jnp.int32, (64, 512), 1) % 8
        for c in range(8):
            picked = jnp.where((classes == wanted) & (column == c), 1.0, 0.0).astype(jnp.bfloat16)
            class_rows[:, 256 * c : 256 * c + 256] = jnp.dot(
                picked, fresh, preferred_element_type=jnp.float32
            ).astype(jnp.bfloat16)
        for k in range(2):
            part = inner_block(class_rows[:, 0:1024], chunks[OWN + 2 * k]) + inner_block(
                class_rows[:, 1024:2048], chunks[OWN + 2 * k + 1]
            )
            score_parts[:, k] = part.astype(jnp.bfloat16).reshape(4, 16, 512)
        for side in range(2):
            score_hop_copy(side).start()

    def score_fold():
        for side in range(2):
            to = lax.rem(x + 1, 4) if side == 0 else lax.rem(x + 3, 4)
            score_hop_copy(side).wait_recv()
            score_parts[to, side] = (
                score_parts[to, side].astype(jnp.float32) + score_hop[side].astype(jnp.float32)
            ).astype(jnp.bfloat16)
            score_fold_copy(side).start()

    def score_finish():
        for side in range(2):
            score_fold_copy(side).wait_recv()
        score_sum[...] = (
            score_parts[x].astype(jnp.float32)
            + score_near[0].astype(jnp.float32)
            + score_near[1].astype(jnp.float32)
        ).astype(jnp.bfloat16)
        score_home_copy().start()

    def place(ref, k, value):
        for xv in range(4):
            ref[:, pl.ds(256 * xv + 128 * k, 128)] = value[:, 128 * xv : 128 * xv + 128].astype(jnp.bfloat16)

    def wide(value):
        return value.astype(jnp.float32)

    def column(xv, k):
        return pl.ds(pl.multiple_of(256 * xv + 128 * k, 128), 128)

    def turn():
        remote(home_self.at[0, :, pl.ds(0, 384)], home_self.at[0, :, pl.ds(0, 384)], home_s.at[0, 0], self_r.at[0], mirror).wait_recv()
        diag = (wide(summed[0, yh, :, 0:384]) + wide(home_self[0, :, 0:384])).astype(jnp.bfloat16)
        for d in range(3):
            self_ref[0, :, column(lax.rem(x + d, 4), yh)] = diag[:, 128 * d : 128 * d + 128]
        turn_out[4] = diag[:, 128:256]
        next_copy().start()

        @pl.when(yh == 0)
        def _():
            beside_home().wait_recv()
            final = wide(summed[1, 0]) + wide(home_self[1])
            place(self_ref.at[0], 1, final)
            for xv in range(4):
                turn_out[xv] = final[:, 128 * xv : 128 * xv + 128].astype(jnp.bfloat16)
                turn_copy(xv).start()

    def turned():
        next_copy().wait_recv()
        self_ref[0, :, column(lax.rem(x + 3, 4), yh)] = wide(turn_in[4]).T.astype(jnp.bfloat16)

        @pl.when(yh == 1)
        def _():
            for xv in range(4):
                remote(turn_in.at[xv], turn_in.at[xv], turn_s.at[xv], turn_r.at[xv], mirror).wait_recv()
                self_ref[0, :, pl.ds(256 * xv, 128)] = wide(turn_in[xv]).T.astype(jnp.bfloat16)

    diagonal()
    compute(1, lambda i: [OWN, OWN + 1], lambda i: [OWN + 2, OWN + 3])
    project()
    pass_on(0)
    fold(0)
    mate_copy(0).wait_recv()

    @pl.when(core == 1)
    def _():
        mate_copy(1).wait_recv()

    theirs = jnp.where(core == 0, MATE, OWN + 2)
    compute(
        2,
        lambda i: [MATE * core + 2 * i, MATE * core + 2 * i + 1],
        lambda i: [theirs, theirs + 1],
    )
    fold(1)
    pass_on(1)
    fold(2)
    pass_on(2)
    pass_on(3)
    piece_inner(0)
    share_first()
    pass_on(4)
    take_along(0)
    piece_along(0)
    fold(3)
    piece_cross(0)
    fold(5)
    pass_on(5)
    fold(7)
    pass_on(6)
    share_second()
    pass_on(7)
    piece_inner(1)
    score_compute()
    finish(0)
    finish(1)
    finish(2)
    take_along(1)
    piece_along(1)
    finish(3)
    fold(4)
    score_fold()
    piece_cross(1)
    finish(5)
    finish(7)
    finish(4)
    fold(6)
    turn()
    score_finish()
    fold(8)
    finish(6)
    finish(8)

    turned()

    @pl.when(core == 0)
    def _():
        within_mirror(0).wait_recv()
        place(cross_ref.at[0, 0], 0, wide(summed[2, yh]) + wide(home_near[0, 0]))
        remote(home_near.at[1, 1], home_near.at[1, 1], home_s.at[2, 0], near_r.at[1, 1], mate).wait_recv()
        remote(home_near.at[2, 1], home_near.at[2, 1], home_s.at[2, 0], near_r.at[2, 1], mate).wait_recv()
        place(cross_ref.at[0, 0], 1, wide(home_near[1, 1]) + wide(home_near[2, 1]))

    mine = jnp.where(yl == 0, 3, 5)

    def gather_home(box, sems, first, out):
        for k in range(2):
            remote(box.at[0, k], box.at[0, k], home_s.at[0, 0], sems.at[0, k], mirror).wait_recv()
        for source in (1, 2):
            for h in range(2):
                remote(
                    box.at[source, h], box.at[source, h], home_s.at[0, 0], sems.at[source, h], mirror
                ).wait_recv()
        for k in range(2):
            place(
                out, k,
                wide(summed[first + k, yh]) + wide(box[0, k]) + wide(box[1, k]) + wide(box[2, k]),
            )

    gather_home(home_far, far_r, mine, cross_ref.at[0, 1])

    @pl.when(core == 1)
    def _():
        gather_home(home_near, near_r, 7, cross_ref.at[0, 0])

    score_home_copy().wait_recv()
    for k in range(2):
        scores = wide(score_sum[k]) + wide(score_home[k])
        place(score_ref, k, jnp.where(yh == 0, scores[0:4], scores[4:8]))

    score_home_copy().wait_send()
    next_copy().wait_send()

    @pl.when(yh == 0)
    def _():
        for xv in range(4):
            turn_copy(xv).wait_send()

    for side in range(2):
        score_hop_copy(side).wait_send()
        score_fold_copy(side).wait_send()
    for step in range(1, 8):
        ring_copy(step).wait_send()
    over_copy().wait_send()
    note_mate_copy().wait_send()
    mate_copy(0).wait_send()

    @pl.when(core == 0)
    def _():
        mate_copy(1).wait_send()

    for step in range(8):
        inner_copy(step).wait_send()
        along_copy(step).wait_send()
    for step in range(8):
        cross_copy(step).wait_send()
    for p in range(PIECES):
        for side in range(2):
            hop_copy(p, side).wait_send()
            for h in range(2):
                fold_copy(p, side, h).wait_send()
            home_op(p, side, lambda copy: copy.wait_send())


def gram_tiles(stored, acts, grads, in_rows, out_rows, classes):
    bf16 = jnp.bfloat16
    dma = pltpu.SemaphoreType.DMA
    return pl.pallas_call(
        tiles_kernel,
        out_shape=(
            jax.ShapeDtypeStruct((1, 128, 1024), bf16),
            jax.ShapeDtypeStruct((1, 2, 128, 1024), bf16),
            jax.ShapeDtypeStruct((4, 1024), bf16),
        ),
        in_specs=[pl.BlockSpec(memory_space=pl.ANY)] * 5 + [pl.BlockSpec(memory_space=pltpu.SMEM)],
        out_specs=(pl.BlockSpec(memory_space=pltpu.VMEM),) * 3,
        scratch_shapes=[
            pltpu.VMEM((14, 512, 1024), bf16),
            pltpu.VMEM((PIECES, 4, 2, 128, 512), bf16),
            pltpu.VMEM((PIECES, 2, 128, 512), bf16),
            pltpu.VMEM((PIECES, 2, 2, 128, 512), bf16),
            pltpu.VMEM((PIECES, 2, 128, 512), bf16),
            pltpu.VMEM((2, 128, 512), bf16),
            pltpu.VMEM((3, 2, 128, 512), bf16),
            pltpu.VMEM((3, 2, 128, 512), bf16),
            pltpu.VMEM((2, 128, 4096), bf16),
            pltpu.VMEM((2, 128, 4096), bf16),
            pltpu.VMEM((2, RANK, 4096), bf16),
            pltpu.VMEM((2, RANK, 4096), bf16),
            pltpu.VMEM((16, 384), jnp.float32),
            pltpu.VMEM((2, 8, 2, 16, 384), bf16),
            pltpu.VMEM((64, 2048), bf16),
            pltpu.VMEM((4, 2, 16, 512), bf16),
            pltpu.VMEM((2, 16, 512), bf16),
            pltpu.VMEM((2, 2, 16, 512), bf16),
            pltpu.VMEM((2, 16, 512), bf16),
            pltpu.VMEM((2, 16, 512), bf16),
            pltpu.VMEM((1024, 2, 1024), bf16),
            pltpu.VMEM((5, 128, 128), bf16),
            pltpu.VMEM((5, 128, 128), bf16),
            dma((5,)), dma((5,)),
            dma((4,)), dma((7,)), dma((7,)), dma((2,)), dma((2,)),
            dma((2,)), dma((2,)), dma((2,)), dma((2,)), dma, dma,
            dma((8,)), dma((2,)), dma((2,)), dma((8,)), dma((8,)), dma((8,)), dma((8,)), dma((8,)), dma((8,)),
            dma((PIECES, 2)), dma((PIECES, 2)), dma((PIECES, 2, 2)), dma((PIECES, 2, 2)), dma((PIECES, 2)),
            dma((2,)), dma((3, 2)), dma((3, 2)),
        ],
        compiler_params=pltpu.CompilerParams(
            collective_id=0, has_side_effects=True, vmem_limit_bytes=56 * 2**20
        ),
        cost_estimate=pl.CostEstimate(flops=13 * 10**9, bytes_accessed=8 * 2**20, transcendentals=0),
        name="gram_tiles",
    )(stored, acts, grads, in_rows, out_rows, classes)


def settle_kernel(*refs):
    for src, dst in zip(refs[0:3], refs[3:6]):
        dst[...] = src[...]


def settle(*results):
    return pl.pallas_call(
        settle_kernel,
        out_shape=tuple(jax.ShapeDtypeStruct(r.shape, r.dtype) for r in results),
        in_specs=[pl.BlockSpec(memory_space=pltpu.VMEM)] * 3,
        out_specs=(pl.BlockSpec(memory_space=pltpu.VMEM),) * 3,
        name="settle",
    )(*results)


def per_device(activations, out_grads, in_factor, out_factor, stored_rows, example_class):
    layer_count = activations.shape[0]
    model_width = activations.shape[3]
    return settle(*gram_tiles(
        stored_rows,
        activations.reshape(layer_count, -1, model_width),
        out_grads.reshape(layer_count, -1, model_width),
        in_factor.transpose(0, 2, 1),
        out_factor.transpose(0, 2, 1),
        example_class,
    ))


def solution(mesh):
    placed = (
        P("layer", "group", None, None),
        P("layer", "group", None, None),
        P("layer", None, None),
        P("layer", None, None),
        P("group", "layer", None),
        P("group"),
    )
    return jax.shard_map(
        per_device,
        mesh=mesh,
        in_specs=placed,
        out_specs=(P("group", "layer", None), P("group", None, "layer", None), P("layer", "group")),
        check_vma=False,
    )
```
